512 devices in a mesh: gx: 8 (over y), gy: 8 (over z_hi, core), gz: 8 (over x, z_lo).
Axes of the slice: x: 4, y: 8, z: 8 (z_hi: 4, z_lo: 2; z = z_hi * 2 + z_lo), core: 2. Of those that a mesh axis runs over, the one named last changes fastest.
Arguments:
- features: bfloat16 [8, 8, 8, 32, 49, 128], P('gx', 'gy', 'gz'), may hold values from -6 to 6
- border_atoms: int32 [8, 8, 8, 4], P('gx', 'gy', 'gz'), may hold values from 0 to 31, as said below
- inner_source: int32 [8, 8, 8, 128], P('gx', 'gy', 'gz'), may hold values from 0 to 31
- inner_target: int32 [8, 8, 8, 128], P('gx', 'gy', 'gz'), may hold values from 0 to 31
- inner_rotation: int32 [8, 8, 8, 128], P('gx', 'gy', 'gz'), may hold values from 0 to 255
- inner_count: int32 [8, 8, 8], P('gx', 'gy', 'gz'), may hold values from 64 to 128, as said below
- cross_source: int32 [8, 8, 8, 128], P('gx', 'gy', 'gz'), may hold values from 0 to 107, as said below
- cross_target: int32 [8, 8, 8, 128], P('gx', 'gy', 'gz'), may hold values from 0 to 31
- cross_rotation: int32 [8, 8, 8, 2, 128], P('gx', 'gy', 'gz'), may hold values from 0 to 255
- cross_count: int32 [8, 8, 8], P('gx', 'gy', 'gz'), may hold values from 64 to 128, as said below
- rotations: bfloat16 [49, 49, 256], replicated, as said below
- order_zero: bfloat16 [896, 896], P(('gy', 'gz')), may hold values from -0.1875 to 0.1875
- order_one: bfloat16 [2, 768, 768], P(None, ('gy', 'gz')), may hold values from -0.15625 to 0.15625
- order_two: bfloat16 [2, 640, 640], P(None, ('gy', 'gz')), may hold values from -0.15625 to 0.15625
Outputs:
- updated: bfloat16 [8, 8, 8, 32, 49, 128], P('gx', 'gy', 'gz')
The draws below stay inside these ranges and needn't reach their ends.
Inputs may be any that keep to these rules, and one draw needn't show every extreme that they name: `border_atoms`: 4 different atoms of the cell. `inner_count`: edges at positions below the count are live; some cell has all 128 live. `cross_count`: edges at positions below the count are live; some cell has all 128 live. `cross_source`: a row s * 4 + t of around with s never 13, the cell itself. An entry rotations[i, j, r] is zero unless i and j have the same degree.
All inputs are finite; a program needn't handle non-finite values.
Results may differ from the reference program's by a relative error of at most 0.006.
Values may be sent and summed in bfloat16 or wider, within the bound.
No kernel may reach another device: no remote copies, remote signals or barrier semaphores. Data moves between devices by JAX's collectives and lax.ppermute only.
A program may use at most 128 MiB of HBM per device.

```python
import jax
import jax.numpy as jnp
import numpy as np
from jax import lax

C = 128
LMAX = 6
ATOMS = 32
BOUND = 4
E_IN = 128
E_X = 128
ROTS = 256
N_GX = 8
N_GY = 8
N_GZ = 8


def live_counts(key, most):
    first_key = jax.random.fold_in(key, 11)
    second_key = jax.random.fold_in(key, 12)
    cell_total = N_GX * N_GY * N_GZ
    counts = jax.random.randint(first_key, (cell_total,), most // 2, most + 1, dtype=jnp.int32)
    fullest = jax.random.randint(second_key, (), 0, cell_total, dtype=jnp.int32)
    counts = counts.at[fullest].set(most)
    return counts.reshape(N_GX, N_GY, N_GZ)


def draw_border_atoms(key, part):
    key = jax.random.fold_in(key, 1)
    scores = jax.random.randint(key, (N_GX, N_GY, N_GZ, ATOMS), 0, 1 << 20, dtype=jnp.int32)
    scores = scores * ATOMS + jnp.arange(ATOMS, dtype=jnp.int32)
    ranked = jnp.argsort(scores, axis=-1, stable=True)
    return ranked[..., :BOUND].astype(jnp.int32)


def draw_inner_count(key, part):
    key = jax.random.fold_in(key, 2)
    return live_counts(key, E_IN)


def draw_cross_count(key, part):
    key = jax.random.fold_in(key, 3)
    return live_counts(key, E_X)


def draw_cross_source(key, part):
    key = jax.random.fold_in(key, 4)
    slot_key = jax.random.fold_in(key, 21)
    atom_key = jax.random.fold_in(key, 22)
    slots = jax.random.randint(slot_key, (N_GX, N_GY, N_GZ, E_X), 0, 26, dtype=jnp.int32)
    slots = slots + (slots >= 13).astype(jnp.int32)
    picked = jax.random.randint(atom_key, (N_GX, N_GY, N_GZ, E_X), 0, BOUND, dtype=jnp.int32)
    return slots * BOUND + picked


def draw_rotations(key, part):
    key = jax.random.fold_in(key, 5)
    harmonics = (LMAX + 1) ** 2
    degree = jnp.asarray(np.array([d for d in range(LMAX + 1) for _ in range(2 * d + 1)], dtype=np.float32))
    same = degree[:, None] == degree[None, :]
    noise = jax.random.normal(key, (harmonics, harmonics, ROTS), jnp.float32)
    column_scale = 0.6 / jnp.sqrt(2.0 * degree + 1.0)
    table = jnp.eye(harmonics, dtype=jnp.float32)[:, :, None] + noise * column_scale[None, :, None]
    table = jnp.where(same[:, :, None], table, 0.0)
    return table.astype(jnp.bfloat16)


def set_ends(drawn, stream_key, least, largest):
    longest = drawn.shape.index(max(drawn.shape))
    spots = []
    for shift in (0, 1):
        where = [jax.random.randint(jax.random.fold_in(stream_key, axis), (), 0, length) for axis, length in enumerate(drawn.shape)]
        where[longest] = (where[longest] + shift) % drawn.shape[longest]
        spots.append(tuple(where))
    return drawn.at[spots[0]].set(least).at[spots[1]].set(largest)


def level_of(own_key, shape, shards, low, largest):
    def one(dim, shards_of):
        steps = jax.random.uniform(jax.random.fold_in(jax.random.fold_in(own_key, 6), dim), (shards_of,), jnp.float32, low / len(shards), largest / len(shards))
        return jnp.repeat(jnp.exp(steps), shape[dim] // shards_of).reshape((-1,) + (1,) * (len(shape) - dim - 1))

    factor_of = one(*shards[0])
    for cut in shards[1:]:
        factor_of = factor_of * one(*cut)
    return factor_of


def centred(stream_key, dims, deviation, limit, cuts=(), kind=jnp.bfloat16):
    values = deviation * jax.random.normal(stream_key, dims, jnp.float32)
    if cuts:
        values = values * level_of(stream_key, dims, cuts, -0.22, 0.18)
    return jnp.clip(values, -limit, limit).astype(kind)


def setup_inputs(seed: int = 0) -> dict:
    seeds = jax.random.split(jax.random.key(seed), 15)
    features = centred(seeds[0], (N_GX, N_GY, N_GZ, ATOMS, (LMAX + 1) ** 2, C), 1.0, 6.0, ((0, 8), (1, 8), (2, 8)))
    border_atoms = draw_border_atoms(jax.random.fold_in(seeds[14], 71), 0)
    inner_source = set_ends(jax.random.randint(seeds[2], (N_GX, N_GY, N_GZ, E_IN), 0, ATOMS), jax.random.fold_in(seeds[2], 1), 0, ATOMS - 1).astype(jnp.int32)
    inner_target = set_ends(jax.random.randint(seeds[3], (N_GX, N_GY, N_GZ, E_IN), 0, ATOMS), jax.random.fold_in(seeds[3], 1), 0, ATOMS - 1).astype(jnp.int32)
    inner_rotation = set_ends(jax.random.randint(seeds[4], (N_GX, N_GY, N_GZ, E_IN), 0, ROTS), jax.random.fold_in(seeds[4], 1), 0, ROTS - 1).astype(jnp.int32)
    inner_count = draw_inner_count(jax.random.fold_in(seeds[14], 71), 0)
    cross_source = draw_cross_source(jax.random.fold_in(seeds[14], 71), 0)
    cross_target = set_ends(jax.random.randint(seeds[7], (N_GX, N_GY, N_GZ, E_X), 0, ATOMS), jax.random.fold_in(seeds[7], 1), 0, ATOMS - 1).astype(jnp.int32)
    cross_rotation = set_ends(jax.random.randint(seeds[8], (N_GX, N_GY, N_GZ, 2, E_X), 0, ROTS), jax.random.fold_in(seeds[8], 1), 0, ROTS - 1).astype(jnp.int32)
    cross_count = draw_cross_count(jax.random.fold_in(seeds[14], 71), 0)
    rotations = draw_rotations(jax.random.fold_in(seeds[14], 71), 0)
    order_zero = centred(seeds[11], ((LMAX + 1) * C, (LMAX + 1) * C), ((LMAX + 1) * C) ** -0.5, 0.1875, ((0, 64),))
    order_one = centred(seeds[12], (2, LMAX * C, LMAX * C), (2 * LMAX * C) ** -0.5, 0.15625, ((1, 64),))
    order_two = centred(seeds[13], (2, (LMAX - 1) * C, (LMAX - 1) * C), (2 * (LMAX - 1) * C) ** -0.5, 0.15625, ((1, 64),))
    return {"features": features, "border_atoms": border_atoms, "inner_source": inner_source, "inner_target": inner_target, "inner_rotation": inner_rotation, "inner_count": inner_count, "cross_source": cross_source, "cross_target": cross_target, "cross_rotation": cross_rotation, "cross_count": cross_count, "rotations": rotations, "order_zero": order_zero, "order_one": order_one, "order_two": order_two}


def kept_rows(top_degree):
    listing = [d * d + d for d in range(top_degree + 1)]
    for shift in (1, -1, 2, -2):
        listing = listing + [d * d + d + shift for d in range(abs(shift), top_degree + 1)]
    return np.array(listing, dtype=np.int32)


def conv_messages(sources, chosen, order_zero, order_one, order_two):
    row_total = sources.shape[0]
    channels = sources.shape[2]
    size_zero = LMAX + 1
    size_one = LMAX
    size_two = LMAX - 1
    turned = jnp.einsum("nrj,njc->nrc", chosen.astype(jnp.float32), sources.astype(jnp.float32)).astype(jnp.bfloat16)
    zero_part = turned[:, :size_zero].reshape(row_total, size_zero * channels)
    plus_one = turned[:, size_zero:size_zero + size_one].reshape(row_total, size_one * channels)
    minus_one = turned[:, size_zero + size_one:size_zero + 2 * size_one].reshape(row_total, size_one * channels)
    two_start = size_zero + 2 * size_one
    plus_two = turned[:, two_start:two_start + size_two].reshape(row_total, size_two * channels)
    minus_two = turned[:, two_start + size_two:two_start + 2 * size_two].reshape(row_total, size_two * channels)
    out_zero = jnp.dot(zero_part, order_zero, preferred_element_type=jnp.float32)
    out_plus1 = jnp.dot(plus_one, order_one[0], preferred_element_type=jnp.float32) - jnp.dot(minus_one, order_one[1], preferred_element_type=jnp.float32)
    out_minus1 = jnp.dot(minus_one, order_one[0], preferred_element_type=jnp.float32) + jnp.dot(plus_one, order_one[1], preferred_element_type=jnp.float32)
    out_plus2 = jnp.dot(plus_two, order_two[0], preferred_element_type=jnp.float32) - jnp.dot(minus_two, order_two[1], preferred_element_type=jnp.float32)
    out_minus2 = jnp.dot(minus_two, order_two[0], preferred_element_type=jnp.float32) + jnp.dot(plus_two, order_two[1], preferred_element_type=jnp.float32)
    pieces = [out_zero, out_plus1, out_minus1, out_plus2, out_minus2]
    mixed = jnp.concatenate([piece.reshape(row_total, -1, channels) for piece in pieces], axis=1).astype(jnp.bfloat16)
    return jnp.einsum("nrj,nrc->njc", chosen.astype(jnp.float32), mixed.astype(jnp.float32))


def reference(features, border_atoms, inner_source, inner_target, inner_rotation, inner_count, cross_source, cross_target, cross_rotation, cross_count, rotations, order_zero, order_one, order_two):
    listing = jnp.asarray(kept_rows(LMAX))
    trimmed = rotations[listing, :, :]
    harmonics = (LMAX + 1) ** 2
    channels = C
    boundary = jnp.take_along_axis(features, border_atoms[..., None, None], axis=3)
    cell_total = N_GX * N_GY * N_GZ
    offsets = jnp.arange(3, dtype=jnp.int32) - 1

    def masked(sources, picked, live):
        live_mask = (jnp.arange(picked.shape[0], dtype=jnp.int32) < live).astype(jnp.float32)
        chosen = jnp.transpose(trimmed[:, :, picked], (2, 0, 1))
        result = conv_messages(sources, chosen, order_zero, order_one, order_two)
        return result * live_mask[:, None, None]

    def one_cell(running, cell):
        cell_x = cell // (N_GY * N_GZ)
        cell_y = (cell // N_GZ) % N_GY
        cell_z = cell % N_GZ
        near_x = (cell_x + offsets) % N_GX
        near_y = (cell_y + offsets) % N_GY
        near_z = (cell_z + offsets) % N_GZ
        beside_all = boundary[near_x[:, None, None], near_y[None, :, None], near_z[None, None, :]]
        beside_all = beside_all.reshape(27 * BOUND, harmonics, channels)
        local_atoms = features[cell_x, cell_y, cell_z]
        inner = masked(local_atoms[inner_source[cell_x, cell_y, cell_z]], inner_rotation[cell_x, cell_y, cell_z], inner_count[cell_x, cell_y, cell_z])
        gathered = jnp.zeros((ATOMS, harmonics, channels), jnp.float32).at[inner_target[cell_x, cell_y, cell_z]].add(inner)
        far_rows = cross_source[cell_x, cell_y, cell_z]
        near_rows = cross_target[cell_x, cell_y, cell_z]
        live = cross_count[cell_x, cell_y, cell_z]
        inward = masked(beside_all[far_rows], cross_rotation[cell_x, cell_y, cell_z, 0], live)
        gathered = gathered.at[near_rows].add(inward)
        outward = masked(local_atoms[near_rows], cross_rotation[cell_x, cell_y, cell_z, 1], live)
        returned = jnp.zeros((27 * BOUND, harmonics, channels), jnp.float32).at[far_rows].add(outward)
        returned = returned.reshape(3, 3, 3, BOUND, harmonics, channels)
        running = running.at[near_x[:, None, None], near_y[None, :, None], near_z[None, None, :]].add(returned)
        return running, gathered

    anchor = jnp.zeros((N_GX, N_GY, N_GZ, BOUND, harmonics, channels), jnp.float32)
    returned_all, gathered_all = lax.scan(one_cell, anchor, jnp.arange(cell_total, dtype=jnp.int32))
    cell_ids = jnp.arange(cell_total, dtype=jnp.int32)[:, None]
    flat_border = border_atoms.reshape(cell_total, BOUND)
    total = gathered_all.at[cell_ids, flat_border].add(returned_all.reshape(cell_total, BOUND, harmonics, channels))
    total = total.reshape(features.shape)
    return (features.astype(jnp.float32) + 0.25 * total).astype(jnp.bfloat16)
```

```python
import functools

import jax
import jax.numpy as jnp
import numpy as np
from jax import lax
from jax.experimental import pallas as pl
from jax.experimental.pallas import tpu as pltpu
from jax.sharding import Mesh
from jax.sharding import PartitionSpec as P

LMAX = 6
HARM = (LMAX + 1) ** 2
JP = 56
KEPT = 29
KP = 32
EDGES = 128
ROTS = 256
ATOMS = 32
BOUND = 4
AROUND = 27 * BOUND
STEP = 32
PITCH = EDGES + 1
LANES = 128
BF16 = jnp.bfloat16
F32 = jnp.float32

SMEM = pl.BlockSpec(memory_space=pltpu.SMEM)
VMEM = pl.BlockSpec(memory_space=pltpu.VMEM)
HBM = pl.BlockSpec(memory_space=pl.ANY)
PARAMS = pltpu.CompilerParams(vmem_limit_bytes=56 * 2**20)

ROWS0, BLK0 = 16, 7
ROWS1, BLK1 = 24, 6
ROWS2, BLK2 = 24, 5
G0 = 4 * ROWS0 * BLK0
G1 = 4 * ROWS1 * BLK1
G2 = 4 * ROWS2 * BLK2
GROWS = G0 + G1 + G2


def kept_rows():
    listing = [d * d + d for d in range(LMAX + 1)]
    for shift in (1, -1, 2, -2):
        listing += [d * d + d + shift for d in range(abs(shift), LMAX + 1)]
    return listing


def slot_order():
    order = []
    for zh in range(4):
        for zl in range(2):
            for core in range(2):
                for x in range(4):
                    order.append(((zh * 2 + core) * 4 + x) * 2 + zl)
    return order


def spreads():
    order = slot_order()
    zero = np.zeros((2, 512, 512), np.float32)
    one = np.zeros((768, 768), np.float32)
    two = np.zeros((2, 768, 768), np.float32)
    for slot, shard in enumerate(order):
        half, local = divmod(slot, 32)
        for r in range(14):
            zero[half, shard * 14 + r - 384 * half, local * ROWS0 + r] = 1
        for r in range(12):
            if half == 0:
                one[shard * 12 + r, local * ROWS1 + r] = 1
                one[384 + shard * 12 + r, local * ROWS1 + 12 + r] = 1
        for r in range(10):
            two[half, shard * 10 + r - 256 * half, local * ROWS2 + r] = 1
            two[half, 384 + shard * 10 + r - 256 * half, local * ROWS2 + 10 + r] = 1
    return [jnp.asarray(m, BF16) for m in (zero, one, two)]


def tables_kernel(border_atoms, feats, x_out, border_out, tmp):
    for j in range(HARM):
        tmp[pl.ds(j * 33, ATOMS), :] = feats[j].astype(F32)
    tail = jnp.zeros((JP - HARM, LANES), F32)
    for a in range(ATOMS):
        rows = tmp[pl.ds(a, HARM, stride=33), :]
        x_out[a] = jnp.concatenate([rows, tail], axis=0).astype(BF16)
    for t in range(BOUND):
        border_out[t] = x_out[border_atoms[t]]


def blocks_of(count):
    return (count + (STEP - 1)) // STEP


def forward_kernel(count, sources, picked, x_ref, rot_ref, sp0, sp1, sp2, t0, t1, t2, tmp):
    def step(s, carry):
        for u in range(STEP):
            e = s * STEP + u
            rows = jnp.dot(rot_ref[picked[e]], x_ref[sources[e]], preferred_element_type=F32)
            tmp[pl.ds(e, KP, stride=PITCH), :] = rows
        return carry

    lax.fori_loop(0, blocks_of(count[0]), step, 0)

    def plane(i):
        return tmp[pl.ds(i * PITCH, EDGES), :].astype(BF16)

    def spread(planes, matrix):
        return jnp.dot(jnp.concatenate(planes, axis=1), matrix, preferred_element_type=F32).astype(BF16)

    zero = [plane(i) for i in range(7)]
    t0[:, 0:512] = spread(zero[0:4], sp0[0])
    t0[:, 512:1024] = spread(zero[3:7], sp0[1])
    plus = [plane(7 + i) for i in range(6)]
    minus = [plane(13 + i) for i in range(6)]
    for h in range(2):
        p, q = plus[3 * h : 3 * h + 3], minus[3 * h : 3 * h + 3]
        t1[0, :, 768 * h : 768 * (h + 1)] = spread(p + [-m for m in q], sp1[...])
        t1[1, :, 768 * h : 768 * (h + 1)] = spread(q + p, sp1[...])
    plus = [plane(19 + i) for i in range(5)]
    minus = [plane(24 + i) for i in range(5)]
    for h in range(2):
        p, q = plus[2 * h : 2 * h + 3], minus[2 * h : 2 * h + 3]
        t2[0, :, 768 * h : 768 * (h + 1)] = spread(p + [-m for m in q], sp2[h])
        t2[1, :, 768 * h : 768 * (h + 1)] = spread(q + p, sp2[h])


def forward(count, sources, picked, x, table, sp):
    return pl.pallas_call(
        forward_kernel,
        out_shape=(
            jax.ShapeDtypeStruct((EDGES, 1024), BF16),
            jax.ShapeDtypeStruct((2, EDGES, 1536), BF16),
            jax.ShapeDtypeStruct((2, EDGES, 1536), BF16),
        ),
        in_specs=[SMEM, SMEM, SMEM, VMEM, VMEM, VMEM, VMEM, VMEM],
        out_specs=(VMEM, VMEM, VMEM),
        scratch_shapes=[pltpu.VMEM((KP * PITCH, LANES), F32)],
        compiler_params=PARAMS,
    )(count, sources, picked, x, table, *sp)


def back_kernel(sets, trash, finish, *refs):
    counts, picked, targets = refs[0:sets], refs[sets : 2 * sets], refs[2 * sets : 3 * sets]
    refs = refs[3 * sets :]
    turned = [refs[3 * i : 3 * i + 3] for i in range(sets)]
    rot_ref, gathered = refs[3 * sets : 3 * sets + 2]
    refs = refs[3 * sets + 2 :]
    outs, (w0, w1, w2, tmp, acc, sems) = refs[:-6], refs[-6:]
    copies = []
    start = 0
    for n, (ref, size) in enumerate(((w0, G0), (w1, G1), (w2, G2))):
        copies.append(pltpu.make_async_copy(gathered.at[:, pl.ds(start, size), :], ref, sems.at[n]))
        copies[-1].start()
        start += size
    acc[...] = jnp.zeros_like(acc)
    for i in range(sets):
        tmp[i, pl.ds(KEPT * PITCH, (KP - KEPT) * PITCH), :] = jnp.zeros(((KP - KEPT) * PITCH, LANES), F32)

    def mix(lhs, ref, rows, blocks, places):
        for b in range(0, blocks, 2):
            width = min(2, blocks - b)
            weight = [
                ref[:, (b + i) * rows : (b + i + 1) * rows, :].reshape(16 * rows, LANES) for i in range(width)
            ]
            weight = jnp.concatenate(weight, axis=1) if width == 2 else weight[0]
            result = jnp.dot(lhs, weight, preferred_element_type=F32)
            for n, (i, first) in enumerate(places):
                for w in range(width):
                    tmp[i, pl.ds((first + b + w) * PITCH, EDGES), :] = result[
                        n * EDGES : (n + 1) * EDGES, w * LANES : (w + 1) * LANES
                    ]

    copies[0].wait()
    mix(
        jnp.concatenate([turned[i][0][...] for i in range(sets)], axis=0),
        w0, 4 * ROWS0, BLK0, [(i, 0) for i in range(sets)],
    )
    for n, (ref, rows, blocks, first) in enumerate(((w1, ROWS1, BLK1, 7), (w2, ROWS2, BLK2, 19))):
        copies[n + 1].wait()
        mix(
            jnp.concatenate([turned[i][n + 1][sign] for i in range(sets) for sign in range(2)], axis=0),
            ref, 4 * rows, blocks, [(i, first + sign * blocks) for i in range(sets) for sign in range(2)],
        )

    for i in range(sets):
        count = counts[i][0]

        def step(s, carry, i=i, count=count):
            for u in range(STEP):
                e = s * STEP + u
                rows = tmp[i, pl.ds(e, KP, stride=PITCH), :].astype(BF16)
                part = lax.dot_general(
                    rot_ref[picked[i][e]], rows, (((0,), (0,)), ((), ())), preferred_element_type=F32
                )
                acc[jnp.where(e < count, targets[i][e], trash)] += part
            return carry

        lax.fori_loop(0, blocks_of(count), step, 0)
    finish(acc, *outs)


def store_returned(acc, low, middle, high):
    low[...] = acc[0:36].astype(BF16)
    middle[...] = acc[36:72]
    high[...] = acc[72:108].astype(BF16)


def store_gathered(acc, out):
    out[...] = acc[0:ATOMS]


def back(counts, picked, targets, turned, table, gathered, rows, trash, finish, out_shape):
    sets = len(counts)
    return pl.pallas_call(
        functools.partial(back_kernel, sets, trash, finish),
        out_shape=out_shape,
        in_specs=[SMEM] * (3 * sets) + [VMEM] * (3 * sets + 1) + [HBM],
        out_specs=jax.tree.map(lambda _: VMEM, out_shape),
        scratch_shapes=[
            pltpu.VMEM((16, G0, LANES), BF16),
            pltpu.VMEM((16, G1, LANES), BF16),
            pltpu.VMEM((16, G2, LANES), BF16),
            pltpu.VMEM((sets, KP * PITCH, LANES), F32),
            pltpu.VMEM((rows, JP, LANES), F32),
            pltpu.SemaphoreType.DMA((3,)),
        ],
        compiler_params=PARAMS,
    )(*counts, *picked, *targets, *[t for one in turned for t in one], table, gathered)


def final_kernel(border_atoms, feats, gathered, returned, out, acc):
    for a in range(ATOMS):
        acc[pl.ds(a * 57, JP), :] = gathered[a]
    for t in range(BOUND):
        acc[pl.ds(border_atoms[t] * 57, JP), :] += returned[t]
    for j in range(HARM):
        total = acc[pl.ds(j, ATOMS, stride=57), :]
        out[j] = (feats[j].astype(F32) + 0.25 * total).astype(BF16)


def ring(axis, block, shift):
    count = lax.axis_size(axis)
    return lax.ppermute(block, axis, [(i, (i + shift) % count) for i in range(count)])


GX, GY, GZ = "gx", ("zh", "core"), ("x", "zl")


def shards(
    features,
    border_atoms,
    inner_source,
    inner_target,
    inner_rotation,
    inner_count,
    cross_source,
    cross_target,
    cross_rotation,
    cross_count,
    rotations,
    order_zero,
    order_one,
    order_two,
):
    share0 = jnp.pad(order_zero.reshape(14, BLK0, LANES).transpose(1, 0, 2), ((0, 0), (0, 2), (0, 0)))
    share1 = order_one.reshape(2, 12, BLK1, LANES).transpose(2, 0, 1, 3).reshape(BLK1, ROWS1, LANES)
    share2 = order_two.reshape(2, 10, BLK2, LANES).transpose(2, 0, 1, 3).reshape(BLK2, 20, LANES)
    share2 = jnp.pad(share2, ((0, 0), (0, ROWS2 - 20), (0, 0)))
    share = jnp.concatenate([s.reshape(-1, LANES) for s in (share0, share1, share2)], axis=0)
    four = lax.all_gather(share, "x", axis=0, tiled=False)
    pieces = []
    start = 0
    for rows, blocks in ((ROWS0, BLK0), (ROWS1, BLK1), (ROWS2, BLK2)):
        piece = four[:, start : start + rows * blocks].reshape(4, blocks, rows, LANES)
        pieces.append(piece.transpose(1, 0, 2, 3).reshape(blocks * 4 * rows, LANES))
        start += rows * blocks
    gathered_weights = lax.all_gather(jnp.concatenate(pieces, axis=0), ("zh", "zl", "core"), axis=0, tiled=False)

    feats = features[0, 0, 0].transpose(1, 0, 2)
    border_rows = border_atoms[0, 0, 0]
    x, border = pl.pallas_call(
        tables_kernel,
        out_shape=(
            jax.ShapeDtypeStruct((ATOMS, JP, LANES), BF16),
            jax.ShapeDtypeStruct((BOUND, JP, LANES), BF16),
        ),
        in_specs=[SMEM, VMEM],
        out_specs=(VMEM, VMEM),
        scratch_shapes=[pltpu.VMEM((HARM * 33, LANES), F32)],
        compiler_params=PARAMS,
    )(border_rows, feats)

    near = border
    for axis in (GX, GY, GZ):
        low = ring(axis, near, 1)
        high = ring(axis, near, -1)
        near = jnp.concatenate([low, near, high], axis=0)
    slot, atom = cross_source[0, 0, 0] // BOUND, cross_source[0, 0, 0] % BOUND
    far_rows = (((slot % 3) * 3 + (slot // 3) % 3) * 3 + slot // 9) * BOUND + atom

    select = np.zeros((KP, HARM), np.float32)
    select[np.arange(KEPT), kept_rows()] = 1
    table = jnp.einsum("ki,ijr->rkj", jnp.asarray(select, BF16), rotations, preferred_element_type=F32)
    table = jnp.pad(table.astype(BF16), ((0, 0), (0, 0), (0, JP - HARM)))

    sp = spreads()
    count_in, count_x = inner_count.reshape(1), cross_count.reshape(1)
    source_in, target_in, rot_in = inner_source[0, 0, 0], inner_target[0, 0, 0], inner_rotation[0, 0, 0]
    source_x, target_x = cross_source[0, 0, 0], cross_target[0, 0, 0]
    rot_inward, rot_outward = cross_rotation[0, 0, 0, 0], cross_rotation[0, 0, 0, 1]
    turned_out = forward(count_x, target_x, rot_outward, x, table, sp)
    turned_in = forward(count_in, source_in, rot_in, x, table, sp)
    turned_x = forward(count_x, far_rows, rot_inward, near, table, sp)

    face = (36, JP, LANES)
    low, middle, high = back(
        [count_x], [rot_outward], [source_x], [turned_out], table, gathered_weights, 112, AROUND, store_returned,
        (jax.ShapeDtypeStruct(face, BF16), jax.ShapeDtypeStruct(face, F32), jax.ShapeDtypeStruct(face, BF16)),
    )
    returned = middle + ring(GX, low, -1).astype(F32) + ring(GX, high, 1).astype(F32)
    for axis in (GY, GZ):
        third = returned.shape[0] // 3
        low = ring(axis, returned[:third].astype(BF16), -1).astype(F32)
        high = ring(axis, returned[2 * third :].astype(BF16), 1).astype(F32)
        returned = returned[third : 2 * third] + low + high

    gathered = back(
        [count_in, count_x], [rot_in, rot_inward], [target_in, target_x], [turned_in, turned_x], table,
        gathered_weights, 40, ATOMS, store_gathered, jax.ShapeDtypeStruct((ATOMS, JP, LANES), F32),
    )

    updated = pl.pallas_call(
        final_kernel,
        out_shape=jax.ShapeDtypeStruct((HARM, ATOMS, LANES), BF16),
        in_specs=[SMEM, VMEM, VMEM, VMEM],
        out_specs=VMEM,
        scratch_shapes=[pltpu.VMEM((ATOMS * 57, LANES), F32)],
        compiler_params=PARAMS,
    )(border_rows, feats, gathered, returned)
    return updated.transpose(1, 0, 2).reshape(features.shape)


def solution(mesh):
    fine = Mesh(mesh.devices.reshape(8, 4, 2, 4, 2), ("gx", "zh", "core", "x", "zl"))
    cell = ("gx", GY, GZ)
    plane = GY + GZ
    in_specs = (
        P(*cell, None, None, None),
        P(*cell, None),
        P(*cell, None),
        P(*cell, None),
        P(*cell, None),
        P(*cell),
        P(*cell, None),
        P(*cell, None),
        P(*cell, None, None),
        P(*cell),
        P(),
        P(plane, None),
        P(None, plane, None),
        P(None, plane, None),
    )
    out_specs = P(*cell, None, None, None)
    return jax.shard_map(shards, mesh=fine, in_specs=in_specs, out_specs=out_specs, check_vma=False)
```

```python
import functools

import jax
import jax.numpy as jnp
import numpy as np
from jax import lax
from jax.experimental import pallas as pl
from jax.experimental.pallas import tpu as pltpu
from jax.sharding import Mesh
from jax.sharding import PartitionSpec as P

LMAX = 6
HARM = (LMAX + 1) ** 2
JP = 56
KEPT = 29
KP = 32
EDGES = 128
ROTS = 256
ATOMS = 32
BOUND = 4
AROUND = 27 * BOUND
STEP = 32
PITCH = EDGES + 1
LANES = 128
BF16 = jnp.bfloat16
F32 = jnp.float32

SMEM = pl.BlockSpec(memory_space=pltpu.SMEM)
VMEM = pl.BlockSpec(memory_space=pltpu.VMEM)
HBM = pl.BlockSpec(memory_space=pltpu.HBM)
ANY = pl.BlockSpec(memory_space=pl.ANY)
PARAMS = pltpu.CompilerParams(vmem_limit_bytes=24 * 2**20)
WIDE = pltpu.CompilerParams(vmem_limit_bytes=58 * 2**20)

ROWS0, BLK0 = 16, 7
ROWS1, BLK1 = 24, 6
ROWS2, BLK2 = 20, 5
G0 = 4 * ROWS0 * BLK0
G1 = 4 * ROWS1 * BLK1
G2 = 4 * ROWS2 * BLK2
GROWS = G0 + G1 + G2


def kept_rows():
    listing = [d * d + d for d in range(LMAX + 1)]
    for shift in (1, -1, 2, -2):
        listing += [d * d + d + shift for d in range(abs(shift), LMAX + 1)]
    return listing


def slot_order():
    order = []
    for zh in range(4):
        for zl in range(2):
            for core in range(2):
                for x in range(4):
                    order.append(((zh * 2 + core) * 4 + x) * 2 + zl)
    return order


def spreads():
    order = slot_order()
    zero = np.zeros((2, 512, 512), np.float32)
    one = np.zeros((768, 768), np.float32)
    two = np.zeros((2, 768, 640), np.float32)
    for slot, shard in enumerate(order):
        half, local = divmod(slot, 32)
        for r in range(14):
            zero[half, shard * 14 + r - 384 * half, local * ROWS0 + r] = 1
        for r in range(12):
            if half == 0:
                one[shard * 12 + r, local * ROWS1 + r] = 1
                one[384 + shard * 12 + r, local * ROWS1 + 12 + r] = 1
        for r in range(10):
            two[half, shard * 10 + r - 256 * half, local * ROWS2 + r] = 1
            two[half, 384 + shard * 10 + r - 256 * half, local * ROWS2 + 10 + r] = 1
    return [jnp.asarray(m, BF16) for m in (zero, one, two)]


def tables_kernel(border_atoms, feats, x_out, border_out, tmp):
    for j in range(HARM):
        tmp[pl.ds(j * 33, ATOMS), :] = feats[j].astype(F32)
    tail = jnp.zeros((JP - HARM, LANES), F32)
    for a in range(ATOMS):
        rows = tmp[pl.ds(a, HARM, stride=33), :]
        x_out[a] = jnp.concatenate([rows, tail], axis=0).astype(BF16)
    for t in range(BOUND):
        border_out[t] = x_out[border_atoms[t]]


def rotations_kernel(rotations, out, tmp):
    blank = jnp.zeros((LANES - HARM, ROTS), F32)
    for n, i in enumerate(kept_rows()):
        rows = jnp.concatenate([rotations[i].astype(F32), blank], axis=0)
        tmp[pl.ds(n, ROTS, stride=KP + 1), :] = rows.T
    for n in range(KEPT, KP):
        tmp[pl.ds(n, ROTS, stride=KP + 1), :] = jnp.zeros((ROTS, LANES), F32)
    for r in range(ROTS):
        out[r] = tmp[pl.ds(r * (KP + 1), KP), 0:JP].astype(BF16)


def blocks_of(count):
    return (count + (STEP - 1)) // STEP


def forward_kernel(sets, *refs):
    counts, sources, picked = refs[0:sets], refs[sets : 2 * sets], refs[2 * sets : 3 * sets]
    x_ref, rot_ref = refs[3 * sets : 3 * sets + 2]
    spread_refs = refs[3 * sets + 2 : 3 * sets + 5]
    outs, (tmp, sp0, sp1, sp2, sems) = refs[3 * sets + 6 : -5], refs[-5:]
    copies = [
        pltpu.make_async_copy(source, target, sems.at[n])
        for n, (source, target) in enumerate(zip(spread_refs, (sp0, sp1, sp2), strict=True))
    ]
    for copy in copies:
        copy.start()

    def spread(planes, matrix):
        return jnp.dot(jnp.concatenate(planes, axis=1), matrix, preferred_element_type=F32).astype(BF16)

    for i in range(sets):
        t0, t1, t2 = outs[3 * i : 3 * i + 3]

        def step(s, carry, i=i):
            for u in range(STEP):
                e = s * STEP + u
                rows = jnp.dot(rot_ref[picked[i][e]], x_ref[sources[i][e]], preferred_element_type=F32)
                tmp[i, pl.ds(e, KP, stride=PITCH), :] = rows
            return carry

        lax.fori_loop(0, blocks_of(counts[i][0]), step, 0)

        def plane(n, i=i):
            return tmp[i, pl.ds(n * PITCH, EDGES), :].astype(BF16)

        if i == 0:
            for copy in copies:
                copy.wait()
        zero = [plane(n) for n in range(7)]
        t0[:, 0:512] = spread(zero[0:4], sp0[0])
        t0[:, 512:1024] = spread(zero[3:7], sp0[1])
        plus = [plane(7 + n) for n in range(6)]
        minus = [plane(13 + n) for n in range(6)]
        for h in range(2):
            p, q = plus[3 * h : 3 * h + 3], minus[3 * h : 3 * h + 3]
            t1[0, :, 768 * h : 768 * (h + 1)] = spread(p + [-m for m in q], sp1[...])
            t1[1, :, 768 * h : 768 * (h + 1)] = spread(q + p, sp1[...])
        plus = [plane(19 + n) for n in range(5)]
        minus = [plane(24 + n) for n in range(5)]
        for h in range(2):
            p, q = plus[2 * h : 2 * h + 3], minus[2 * h : 2 * h + 3]
            t2[0, :, 640 * h : 640 * (h + 1)] = spread(p + [-m for m in q], sp2[h])
            t2[1, :, 640 * h : 640 * (h + 1)] = spread(q + p, sp2[h])


def forward(counts, sources, picked, x, table, sp, after):
    sets = len(counts)
    one = (
        jax.ShapeDtypeStruct((EDGES, 64 * ROWS0), BF16),
        jax.ShapeDtypeStruct((2, EDGES, 64 * ROWS1), BF16),
        jax.ShapeDtypeStruct((2, EDGES, 64 * ROWS2), BF16),
    )
    outs = pl.pallas_call(
        functools.partial(forward_kernel, sets),
        out_shape=one * sets,
        in_specs=[SMEM] * (3 * sets) + [VMEM] * 2 + [HBM] * 3 + [ANY],
        out_specs=(VMEM,) * (3 * sets),
        scratch_shapes=[pltpu.VMEM((sets, KP * PITCH, LANES), F32)]
        + [pltpu.VMEM(m.shape, BF16) for m in sp]
        + [pltpu.SemaphoreType.DMA((3,))],
        compiler_params=WIDE,
    )(*counts, *sources, *picked, x, table, *sp, after)
    return [outs[3 * i : 3 * i + 3] for i in range(sets)]


def back_kernel(sets, trash, finish, *refs):
    counts, picked, targets = refs[0:sets], refs[sets : 2 * sets], refs[2 * sets : 3 * sets]
    refs = refs[3 * sets :]
    sources = [refs[3 * i : 3 * i + 3] for i in range(sets)]
    table, gathered, _ = refs[3 * sets : 3 * sets + 3]
    refs = refs[3 * sets + 3 :]
    outs, (w0, w1, w2, t0, t1, t2, rot_ref, tmp, acc, sems) = refs[:-10], refs[-10:]
    moves = []
    start = 0
    for n, (weight, turned, size) in enumerate(((w0, t0, G0), (w1, t1, G1), (w2, t2, G2))):
        moves.append([(sources[i][n], turned.at[i]) for i in range(sets)])
        moves[-1].append((gathered.at[:, pl.ds(start, size), :], weight))
        start += size
    moves.append([(table, rot_ref)])
    copies = []
    for n, group in enumerate(moves):
        copies.append(
            [pltpu.make_async_copy(src, dst, sems.at[n, m]) for m, (src, dst) in enumerate(group)]
        )
        for copy in copies[-1]:
            copy.start()

    def arrived(n):
        for copy in copies[n]:
            copy.wait()

    acc[...] = jnp.zeros_like(acc)
    for i in range(sets):
        tmp[i, pl.ds(KEPT * PITCH, (KP - KEPT) * PITCH), :] = jnp.zeros(((KP - KEPT) * PITCH, LANES), F32)

    def mix(lhs, ref, rows, blocks, places):
        for b in range(0, blocks, 2):
            width = min(2, blocks - b)
            weight = [
                ref[:, (b + i) * rows : (b + i + 1) * rows, :].reshape(16 * rows, LANES) for i in range(width)
            ]
            weight = jnp.concatenate(weight, axis=1) if width == 2 else weight[0]
            result = jnp.dot(lhs, weight, preferred_element_type=F32)
            for n, (i, first) in enumerate(places):
                for w in range(width):
                    tmp[i, pl.ds((first + b + w) * PITCH, EDGES), :] = result[
                        n * EDGES : (n + 1) * EDGES, w * LANES : (w + 1) * LANES
                    ]

    arrived(0)
    mix(t0[...].reshape(sets * EDGES, 64 * ROWS0), w0, 4 * ROWS0, BLK0, [(i, 0) for i in range(sets)])
    for n, (lhs, ref, rows, blocks, first) in enumerate(((t1, w1, ROWS1, BLK1, 7), (t2, w2, ROWS2, BLK2, 19))):
        arrived(n + 1)
        mix(
            lhs[...].reshape(sets * 2 * EDGES, 64 * rows), ref, 4 * rows, blocks,
            [(i, first + sign * blocks) for i in range(sets) for sign in range(2)],
        )
    arrived(3)

    for i in range(sets):
        count = counts[i][0]

        def step(s, carry, i=i, count=count):
            for u in range(STEP):
                e = s * STEP + u
                rows = tmp[i, pl.ds(e, KP, stride=PITCH), :].astype(BF16)
                part = lax.dot_general(
                    rot_ref[picked[i][e]], rows, (((0,), (0,)), ((), ())), preferred_element_type=F32
                )
                acc[jnp.where(e < count, targets[i][e], trash)] += part
            return carry

        lax.fori_loop(0, blocks_of(count), step, 0)
    finish(acc, *outs)


def store_returned(acc, low, middle, high):
    low[...] = acc[0:36].astype(BF16)
    middle[...] = acc[36:72]
    high[...] = acc[72:108].astype(BF16)


def store_gathered(acc, out):
    out[...] = acc[0:ATOMS]


def back(counts, picked, targets, turned, table, gathered, after, rows, trash, finish, out_shape):
    sets = len(counts)
    return pl.pallas_call(
        functools.partial(back_kernel, sets, trash, finish),
        out_shape=out_shape,
        in_specs=[SMEM] * (3 * sets) + [HBM] * (3 * sets + 2) + [ANY],
        out_specs=jax.tree.map(lambda _: VMEM, out_shape),
        scratch_shapes=[
            pltpu.VMEM((16, G0, LANES), BF16),
            pltpu.VMEM((16, G1, LANES), BF16),
            pltpu.VMEM((16, G2, LANES), BF16),
            pltpu.VMEM((sets, EDGES, 64 * ROWS0), BF16),
            pltpu.VMEM((sets, 2, EDGES, 64 * ROWS1), BF16),
            pltpu.VMEM((sets, 2, EDGES, 64 * ROWS2), BF16),
            pltpu.VMEM((ROTS, KP, JP), BF16),
            pltpu.VMEM((sets, KP * PITCH, LANES), F32),
            pltpu.VMEM((rows, JP, LANES), F32),
            pltpu.SemaphoreType.DMA((4, sets + 1)),
        ],
        compiler_params=WIDE,
    )(*counts, *picked, *targets, *[t for one in turned for t in one], table, gathered, after)


def final_kernel(border_atoms, feats, gathered_in, gathered_x, returned, out, acc):
    for a in range(ATOMS):
        acc[pl.ds(a * 57, JP), :] = gathered_in[a] + gathered_x[a]
    for t in range(BOUND):
        acc[pl.ds(border_atoms[t] * 57, JP), :] += returned[t]
    for j in range(HARM):
        total = acc[pl.ds(j, ATOMS, stride=57), :]
        out[j] = (feats[j].astype(F32) + 0.25 * total).astype(BF16)


def ring(axis, block, shift):
    count = lax.axis_size(axis)
    return lax.ppermute(block, axis, [(i, (i + shift) % count) for i in range(count)])


GX, GY, GZ = "gx", ("zh", "core"), ("x", "zl")


def shards(
    features,
    border_atoms,
    inner_source,
    inner_target,
    inner_rotation,
    inner_count,
    cross_source,
    cross_target,
    cross_rotation,
    cross_count,
    rotations,
    order_zero,
    order_one,
    order_two,
):
    share0 = jnp.pad(order_zero.reshape(14, BLK0, LANES).transpose(1, 0, 2), ((0, 0), (0, 2), (0, 0)))
    share1 = order_one.reshape(2, 12, BLK1, LANES).transpose(2, 0, 1, 3).reshape(BLK1, ROWS1, LANES)
    share2 = order_two.reshape(2, 10, BLK2, LANES).transpose(2, 0, 1, 3).reshape(BLK2, 20, LANES)
    share = jnp.concatenate([s.reshape(-1, LANES) for s in (share0, share1, share2)], axis=0)
    four = lax.all_gather(share, "x", axis=0, tiled=False)
    pieces = []
    start = 0
    for rows, blocks in ((ROWS0, BLK0), (ROWS1, BLK1), (ROWS2, BLK2)):
        piece = four[:, start : start + rows * blocks].reshape(4, blocks, rows, LANES)
        pieces.append(piece.transpose(1, 0, 2, 3).reshape(blocks * 4 * rows, LANES))
        start += rows * blocks
    gathered_weights = lax.all_gather(jnp.concatenate(pieces, axis=0), ("zh", "zl", "core"), axis=0, tiled=False)

    feats = features[0, 0, 0].transpose(1, 0, 2)
    border_rows = border_atoms[0, 0, 0]
    x, border = pl.pallas_call(
        tables_kernel,
        out_shape=(
            jax.ShapeDtypeStruct((ATOMS, JP, LANES), BF16),
            jax.ShapeDtypeStruct((BOUND, JP, LANES), BF16),
        ),
        in_specs=[SMEM, VMEM],
        out_specs=(VMEM, VMEM),
        scratch_shapes=[pltpu.VMEM((HARM * 33, LANES), F32)],
        compiler_params=PARAMS,
    )(border_rows, feats)

    table = pl.pallas_call(
        rotations_kernel,
        out_shape=jax.ShapeDtypeStruct((ROTS, KP, JP), BF16),
        in_specs=[VMEM],
        out_specs=VMEM,
        scratch_shapes=[pltpu.VMEM((ROTS * (KP + 1), LANES), F32)],
        compiler_params=pltpu.CompilerParams(vmem_limit_bytes=12 * 2**20),
    )(rotations)

    sp = spreads()
    count_in, count_x = inner_count.reshape(1), cross_count.reshape(1)
    source_in, target_in, rot_in = inner_source[0, 0, 0], inner_target[0, 0, 0], inner_rotation[0, 0, 0]
    far_rows, target_x = cross_source[0, 0, 0], cross_target[0, 0, 0]
    rot_inward, rot_outward = cross_rotation[0, 0, 0, 0], cross_rotation[0, 0, 0, 1]

    def widen(axis, block):
        return jnp.concatenate([ring(axis, block, 1), block, ring(axis, block, -1)], axis=0)

    near = widen(GZ, border)
    turned_out, turned_in = forward(
        [count_x, count_in], [target_x, source_in], [rot_outward, rot_in], x, table, sp, near
    )
    near = widen(GY, near)
    near, turned_in = lax.optimization_barrier((near, turned_in))
    near = widen(GX, near)

    face = (36, JP, LANES)
    inside = (ATOMS, JP, LANES)
    low, middle, high = back(
        [count_x], [rot_outward], [far_rows], [turned_out], table, gathered_weights, near, 112, AROUND,
        store_returned,
        (jax.ShapeDtypeStruct(face, BF16), jax.ShapeDtypeStruct(face, F32), jax.ShapeDtypeStruct(face, BF16)),
    )

    def fold(axis, low, middle, high):
        return middle + ring(axis, low, -1).astype(F32) + ring(axis, high, 1).astype(F32)

    def thirds(block):
        third = block.shape[0] // 3
        return block[:third].astype(BF16), block[third : 2 * third], block[2 * third :].astype(BF16)

    gathered_in = back(
        [count_in], [rot_in], [target_in], [turned_in], table, gathered_weights, low, 40, ATOMS, store_gathered,
        jax.ShapeDtypeStruct(inside, F32),
    )
    [turned_x] = forward([count_x], [far_rows], [rot_inward], near, table, sp, gathered_in)
    returned = fold(GX, low, middle, high)
    returned, turned_x = lax.optimization_barrier((returned, turned_x))
    gathered_x = back(
        [count_x], [rot_inward], [target_x], [turned_x], table, gathered_weights, returned, 40, ATOMS,
        store_gathered, jax.ShapeDtypeStruct(inside, F32),
    )
    returned = fold(GY, *thirds(returned))
    returned, gathered_x = lax.optimization_barrier((returned, gathered_x))
    returned = fold(GZ, *thirds(returned))

    updated = pl.pallas_call(
        final_kernel,
        out_shape=jax.ShapeDtypeStruct((HARM, ATOMS, LANES), BF16),
        in_specs=[SMEM] + [VMEM] * 4,
        out_specs=VMEM,
        scratch_shapes=[pltpu.VMEM((ATOMS * 57, LANES), F32)],
        compiler_params=PARAMS,
    )(border_rows, feats, gathered_in, gathered_x, returned)
    return updated.transpose(1, 0, 2).reshape(features.shape)


def solution(mesh):
    fine = Mesh(mesh.devices.reshape(8, 4, 2, 4, 2), ("gx", "zh", "core", "x", "zl"))
    cell = ("gx", GY, GZ)
    plane = GY + GZ
    in_specs = (
        P(*cell, None, None, None),
        P(*cell, None),
        P(*cell, None),
        P(*cell, None),
        P(*cell, None),
        P(*cell),
        P(*cell, None),
        P(*cell, None),
        P(*cell, None, None),
        P(*cell),
        P(),
        P(plane, None),
        P(None, plane, None),
        P(None, plane, None),
    )
    out_specs = P(*cell, None, None, None)
    return jax.shard_map(shards, mesh=fine, in_specs=in_specs, out_specs=out_specs, check_vma=False)
```

```python
import functools

import jax
import jax.numpy as jnp
import numpy as np
from jax import lax
from jax.experimental import pallas as pl
from jax.experimental.pallas import tpu as pltpu
from jax.sharding import Mesh
from jax.sharding import PartitionSpec as P

LMAX = 6
HARM = (LMAX + 1) ** 2
JP = 56
KEPT = 29
KP = 32
EDGES = 128
ROTS = 256
ATOMS = 32
BOUND = 4
AROUND = 27 * BOUND
STEP = 32
PITCH = EDGES + 1
LANES = 128
BF16 = jnp.bfloat16
F32 = jnp.float32

SMEM = pl.BlockSpec(memory_space=pltpu.SMEM)
VMEM = pl.BlockSpec(memory_space=pltpu.VMEM)
HBM = pl.BlockSpec(memory_space=pltpu.HBM)
ANY = pl.BlockSpec(memory_space=pl.ANY)
PARAMS = pltpu.CompilerParams(vmem_limit_bytes=24 * 2**20)
WIDE = pltpu.CompilerParams(vmem_limit_bytes=58 * 2**20)

ROWS0, BLK0 = 16, 7
ROWS1, BLK1 = 24, 6
ROWS2, BLK2 = 20, 5
G0 = 4 * ROWS0 * BLK0
G1 = 4 * ROWS1 * BLK1
G2 = 4 * ROWS2 * BLK2
GROWS = G0 + G1 + G2


def kept_rows():
    listing = [d * d + d for d in range(LMAX + 1)]
    for shift in (1, -1, 2, -2):
        listing += [d * d + d + shift for d in range(abs(shift), LMAX + 1)]
    return listing


def slot_order():
    order = []
    for zh in range(4):
        for zl in range(2):
            for core in range(2):
                for x in range(4):
                    order.append(((zh * 2 + core) * 4 + x) * 2 + zl)
    return order


def spreads():
    order = slot_order()
    zero = np.zeros((2, 512, 512), np.float32)
    one = np.zeros((768, 768), np.float32)
    two = np.zeros((2, 768, 640), np.float32)
    for slot, shard in enumerate(order):
        half, local = divmod(slot, 32)
        for r in range(14):
            zero[half, shard * 14 + r - 384 * half, local * ROWS0 + r] = 1
        for r in range(12):
            if half == 0:
                one[shard * 12 + r, local * ROWS1 + r] = 1
                one[384 + shard * 12 + r, local * ROWS1 + 12 + r] = 1
        for r in range(10):
            two[half, shard * 10 + r - 256 * half, local * ROWS2 + r] = 1
            two[half, 384 + shard * 10 + r - 256 * half, local * ROWS2 + 10 + r] = 1
    return [jnp.asarray(m, BF16) for m in (zero, one, two)]


def tables_kernel(border_atoms, feats, x_out, border_out, tmp):
    for j in range(HARM):
        tmp[pl.ds(j * 33, ATOMS), :] = feats[j].astype(F32)
    tail = jnp.zeros((JP - HARM, LANES), F32)
    for a in range(ATOMS):
        rows = tmp[pl.ds(a, HARM, stride=33), :]
        x_out[a] = jnp.concatenate([rows, tail], axis=0).astype(BF16)
    for t in range(BOUND):
        border_out[t] = x_out[border_atoms[t]]


def rotations_kernel(rotations, out, tmp):
    blank = jnp.zeros((LANES - HARM, ROTS), F32)
    for n, i in enumerate(kept_rows()):
        rows = jnp.concatenate([rotations[i].astype(F32), blank], axis=0)
        tmp[pl.ds(n, ROTS, stride=KP + 1), :] = rows.T
    for n in range(KEPT, KP):
        tmp[pl.ds(n, ROTS, stride=KP + 1), :] = jnp.zeros((ROTS, LANES), F32)
    for r in range(ROTS):
        out[r] = tmp[pl.ds(r * (KP + 1), KP), 0:JP].astype(BF16)


def blocks_of(count):
    return (count + (STEP - 1)) // STEP


def forward_kernel(sets, parts, *refs):
    counts, sources, picked = refs[0:sets], refs[sets : 2 * sets], refs[2 * sets : 3 * sets]
    refs = refs[3 * sets :]
    part_refs, table, spread_refs = refs[0:parts], refs[parts], refs[parts + 1 : parts + 4]
    outs, (tmp, x_ref, rot_ref, sp0, sp1, sp2, sems) = refs[parts + 5 : -7], refs[-7:]
    rows = x_ref.shape[0] // parts
    moves = [(part, x_ref.at[pl.ds(n * rows, rows)]) for n, part in enumerate(part_refs)]
    moves += [(table, rot_ref), *zip(spread_refs, (sp0, sp1, sp2), strict=True)]
    copies = [pltpu.make_async_copy(src, dst, sems.at[n]) for n, (src, dst) in enumerate(moves)]
    for copy in copies:
        copy.start()
    for copy in copies[:-3]:
        copy.wait()

    def spread(planes, matrix):
        return jnp.dot(jnp.concatenate(planes, axis=1), matrix, preferred_element_type=F32).astype(BF16)

    for i in range(sets):
        t0, t1, t2 = outs[3 * i : 3 * i + 3]

        def step(s, carry, i=i):
            for u in range(STEP):
                e = s * STEP + u
                rows = jnp.dot(rot_ref[picked[i][e]], x_ref[sources[i][e]], preferred_element_type=F32)
                tmp[i, pl.ds(e, KP, stride=PITCH), :] = rows
            return carry

        lax.fori_loop(0, blocks_of(counts[i][0]), step, 0)

        def plane(n, i=i):
            return tmp[i, pl.ds(n * PITCH, EDGES), :].astype(BF16)

        if i == 0:
            for copy in copies[-3:]:
                copy.wait()
        zero = [plane(n) for n in range(7)]
        t0[:, 0:512] = spread(zero[0:4], sp0[0])
        t0[:, 512:1024] = spread(zero[3:7], sp0[1])
        plus = [plane(7 + n) for n in range(6)]
        minus = [plane(13 + n) for n in range(6)]
        for h in range(2):
            p, q = plus[3 * h : 3 * h + 3], minus[3 * h : 3 * h + 3]
            t1[0, :, 768 * h : 768 * (h + 1)] = spread(p + [-m for m in q], sp1[...])
            t1[1, :, 768 * h : 768 * (h + 1)] = spread(q + p, sp1[...])
        plus = [plane(19 + n) for n in range(5)]
        minus = [plane(24 + n) for n in range(5)]
        for h in range(2):
            p, q = plus[2 * h : 2 * h + 3], minus[2 * h : 2 * h + 3]
            t2[0, :, 640 * h : 640 * (h + 1)] = spread(p + [-m for m in q], sp2[h])
            t2[1, :, 640 * h : 640 * (h + 1)] = spread(q + p, sp2[h])


def forward(counts, sources, picked, parts, table, sp, after):
    sets = len(counts)
    one = (
        jax.ShapeDtypeStruct((EDGES, 64 * ROWS0), BF16),
        jax.ShapeDtypeStruct((2, EDGES, 64 * ROWS1), BF16),
        jax.ShapeDtypeStruct((2, EDGES, 64 * ROWS2), BF16),
    )
    outs = pl.pallas_call(
        functools.partial(forward_kernel, sets, len(parts)),
        out_shape=one * sets,
        in_specs=[SMEM] * (3 * sets) + [HBM] * (len(parts) + 4) + [ANY],
        out_specs=(VMEM,) * (3 * sets),
        scratch_shapes=[
            pltpu.VMEM((sets, KP * PITCH, LANES), F32),
            pltpu.VMEM((len(parts) * parts[0].shape[0], JP, LANES), BF16),
            pltpu.VMEM((ROTS, KP, JP), BF16),
        ]
        + [pltpu.VMEM(m.shape, BF16) for m in sp]
        + [pltpu.SemaphoreType.DMA((len(parts) + 4,))],
        compiler_params=WIDE,
    )(*counts, *sources, *picked, *parts, table, *sp, after)
    return [outs[3 * i : 3 * i + 3] for i in range(sets)]


def back_kernel(sets, trash, finish, *refs):
    counts, picked, targets = refs[0:sets], refs[sets : 2 * sets], refs[2 * sets : 3 * sets]
    refs = refs[3 * sets :]
    sources = [refs[3 * i : 3 * i + 3] for i in range(sets)]
    table, gathered, _ = refs[3 * sets : 3 * sets + 3]
    refs = refs[3 * sets + 3 :]
    outs, (w0, w1, w2, t0, t1, t2, rot_ref, tmp, acc, sems) = refs[:-10], refs[-10:]
    moves = []
    start = 0
    for n, (weight, turned, size) in enumerate(((w0, t0, G0), (w1, t1, G1), (w2, t2, G2))):
        moves.append([(sources[i][n], turned.at[i]) for i in range(sets)])
        moves[-1].append((gathered.at[:, pl.ds(start, size), :], weight))
        start += size
    moves.append([(table, rot_ref)])
    copies = []
    for n, group in enumerate(moves):
        copies.append(
            [pltpu.make_async_copy(src, dst, sems.at[n, m]) for m, (src, dst) in enumerate(group)]
        )
        for copy in copies[-1]:
            copy.start()

    def arrived(n):
        for copy in copies[n]:
            copy.wait()

    acc[...] = jnp.zeros_like(acc)
    for i in range(sets):
        tmp[i, pl.ds(KEPT * PITCH, (KP - KEPT) * PITCH), :] = jnp.zeros(((KP - KEPT) * PITCH, LANES), F32)

    def mix(lhs, ref, rows, blocks, places):
        for b in range(0, blocks, 2):
            width = min(2, blocks - b)
            weight = [
                ref[:, (b + i) * rows : (b + i + 1) * rows, :].reshape(16 * rows, LANES) for i in range(width)
            ]
            weight = jnp.concatenate(weight, axis=1) if width == 2 else weight[0]
            result = jnp.dot(lhs, weight, preferred_element_type=F32)
            for n, (i, first) in enumerate(places):
                for w in range(width):
                    tmp[i, pl.ds((first + b + w) * PITCH, EDGES), :] = result[
                        n * EDGES : (n + 1) * EDGES, w * LANES : (w + 1) * LANES
                    ]

    arrived(0)
    mix(t0[...].reshape(sets * EDGES, 64 * ROWS0), w0, 4 * ROWS0, BLK0, [(i, 0) for i in range(sets)])
    for n, (lhs, ref, rows, blocks, first) in enumerate(((t1, w1, ROWS1, BLK1, 7), (t2, w2, ROWS2, BLK2, 19))):
        arrived(n + 1)
        mix(
            lhs[...].reshape(sets * 2 * EDGES, 64 * rows), ref, 4 * rows, blocks,
            [(i, first + sign * blocks) for i in range(sets) for sign in range(2)],
        )
    arrived(3)

    for i in range(sets):
        count = counts[i][0]

        def step(s, carry, i=i, count=count):
            for u in range(STEP):
                e = s * STEP + u
                rows = tmp[i, pl.ds(e, KP, stride=PITCH), :].astype(BF16)
                part = lax.dot_general(
                    rot_ref[picked[i][e]], rows, (((0,), (0,)), ((), ())), preferred_element_type=F32
                )
                acc[jnp.where(e < count, targets[i][e], trash)] += part
            return carry

        lax.fori_loop(0, blocks_of(count), step, 0)
    finish(acc, *outs)


def store_returned(acc, first, middle, last):
    first[...] = acc[0:36].astype(BF16)
    middle[...] = acc[36:72]
    last[...] = acc[72:108].astype(BF16)


def store_gathered(acc, out):
    out[...] = acc[0:ATOMS]


def back(counts, picked, targets, turned, table, gathered, after, rows, trash, finish, out_shape):
    sets = len(counts)
    return pl.pallas_call(
        functools.partial(back_kernel, sets, trash, finish),
        out_shape=out_shape,
        in_specs=[SMEM] * (3 * sets) + [HBM] * (3 * sets + 2) + [ANY],
        out_specs=jax.tree.map(lambda _: VMEM, out_shape),
        scratch_shapes=[
            pltpu.VMEM((16, G0, LANES), BF16),
            pltpu.VMEM((16, G1, LANES), BF16),
            pltpu.VMEM((16, G2, LANES), BF16),
            pltpu.VMEM((sets, EDGES, 64 * ROWS0), BF16),
            pltpu.VMEM((sets, 2, EDGES, 64 * ROWS1), BF16),
            pltpu.VMEM((sets, 2, EDGES, 64 * ROWS2), BF16),
            pltpu.VMEM((ROTS, KP, JP), BF16),
            pltpu.VMEM((sets, KP * PITCH, LANES), F32),
            pltpu.VMEM((rows, JP, LANES), F32),
            pltpu.SemaphoreType.DMA((4, sets + 1)),
        ],
        compiler_params=WIDE,
    )(*counts, *picked, *targets, *[t for one in turned for t in one], table, gathered, after)


def final_kernel(border_atoms, feats, gathered, returned, out, acc):
    for a in range(ATOMS):
        acc[pl.ds(a * 57, JP), :] = gathered[a]
    for t in range(BOUND):
        acc[pl.ds(border_atoms[t] * 57, JP), :] += returned[t]
    for j in range(HARM):
        total = acc[pl.ds(j, ATOMS, stride=57), :]
        out[j] = (feats[j].astype(F32) + 0.25 * total).astype(BF16)


def swap(axis, block, odd):
    count = lax.axis_size(axis)
    return lax.ppermute(block, axis, [(i, (i + (1 if (i + odd) % 2 == 0 else -1)) % count) for i in range(count)])


def exchange(axis, first, last):
    last = swap(axis, last, 1)
    if axis == GY:
        both = lax.all_gather(first, "core", axis=0, tiled=False)
        return jnp.where(lax.axis_index("core") == 0, both[1], both[0]), last
    return swap(axis, first, 0), last


def widen(axis, block):
    first, last = exchange(axis, block, block)
    return jnp.concatenate([first, block, last], axis=0)


def fold(axis, first, middle, last):
    first, last = exchange(axis, first, last)
    return middle + first.astype(F32) + last.astype(F32)


def thirds(block):
    third = block.shape[0] // 3
    return block[:third].astype(BF16), block[third : 2 * third], block[2 * third :].astype(BF16)


GX, GY, GZ = "gx", ("zh", "core"), ("x", "zl")


def shards(
    features,
    border_atoms,
    inner_source,
    inner_target,
    inner_rotation,
    inner_count,
    cross_source,
    cross_target,
    cross_rotation,
    cross_count,
    rotations,
    order_zero,
    order_one,
    order_two,
):
    share0 = jnp.pad(order_zero.reshape(14, BLK0, LANES).transpose(1, 0, 2), ((0, 0), (0, 2), (0, 0)))
    share1 = order_one.reshape(2, 12, BLK1, LANES).transpose(2, 0, 1, 3).reshape(BLK1, ROWS1, LANES)
    share2 = order_two.reshape(2, 10, BLK2, LANES).transpose(2, 0, 1, 3).reshape(BLK2, 20, LANES)
    share = jnp.concatenate([s.reshape(-1, LANES) for s in (share0, share1, share2)], axis=0)
    four = lax.all_gather(share, "x", axis=0, tiled=False)
    pieces = []
    start = 0
    for rows, blocks in ((ROWS0, BLK0), (ROWS1, BLK1), (ROWS2, BLK2)):
        piece = four[:, start : start + rows * blocks].reshape(4, blocks, rows, LANES)
        pieces.append(piece.transpose(1, 0, 2, 3).reshape(blocks * 4 * rows, LANES))
        start += rows * blocks
    gathered_weights = lax.all_gather(jnp.concatenate(pieces, axis=0), ("zh", "zl", "core"), axis=0, tiled=False)

    feats = features[0, 0, 0].transpose(1, 0, 2)
    border_rows = border_atoms[0, 0, 0]
    x, border = pl.pallas_call(
        tables_kernel,
        out_shape=(
            jax.ShapeDtypeStruct((ATOMS, JP, LANES), BF16),
            jax.ShapeDtypeStruct((BOUND, JP, LANES), BF16),
        ),
        in_specs=[SMEM, VMEM],
        out_specs=(VMEM, VMEM),
        scratch_shapes=[pltpu.VMEM((HARM * 33, LANES), F32)],
        compiler_params=PARAMS,
    )(border_rows, feats)

    table = pl.pallas_call(
        rotations_kernel,
        out_shape=jax.ShapeDtypeStruct((ROTS, KP, JP), BF16),
        in_specs=[VMEM],
        out_specs=VMEM,
        scratch_shapes=[pltpu.VMEM((ROTS * (KP + 1), LANES), F32)],
        compiler_params=pltpu.CompilerParams(vmem_limit_bytes=12 * 2**20),
    )(rotations)

    sp = spreads()
    count_in, count_x = inner_count.reshape(1), cross_count.reshape(1)
    source_in, target_in, rot_in = inner_source[0, 0, 0], inner_target[0, 0, 0], inner_rotation[0, 0, 0]
    far_rows, target_x = cross_source[0, 0, 0], cross_target[0, 0, 0]
    rot_inward, rot_outward = cross_rotation[0, 0, 0, 0], cross_rotation[0, 0, 0, 1]
    def place(axis, offset):
        return jnp.where(lax.axis_index(axis) % 2 == 1, offset, 2 - offset)

    slot, atom = far_rows // BOUND, far_rows % BOUND
    far_rows = (place(GX, slot // 9) * 3 + place(GY, slot // 3 % 3)) * 3 + place(GZ, slot % 3)
    far_rows = far_rows * BOUND + atom

    near = widen(GZ, border)
    [turned_out] = forward([count_x], [target_x], [rot_outward], [x], table, sp, near)
    near = widen(GY, near)
    near, turned_out = lax.optimization_barrier((near, turned_out))
    near_first, near_last = exchange(GX, near, near)
    [turned_in] = forward([count_in], [source_in], [rot_in], [x], table, sp, near)
    [turned_x] = forward(
        [count_x], [far_rows], [rot_inward], [near_first, near, near_last], table, sp, turned_in[0]
    )

    face = (36, JP, LANES)
    first, middle, last = back(
        [count_x], [rot_outward], [far_rows], [turned_out], table, gathered_weights, turned_x[0], 112, AROUND,
        store_returned,
        (jax.ShapeDtypeStruct(face, BF16), jax.ShapeDtypeStruct(face, F32), jax.ShapeDtypeStruct(face, BF16)),
    )
    gathered = back(
        [count_in, count_x], [rot_in, rot_inward], [target_in, target_x], [turned_in, turned_x], table,
        gathered_weights, first, 40, ATOMS, store_gathered, jax.ShapeDtypeStruct((ATOMS, JP, LANES), F32),
    )
    returned = fold(GX, first, middle, last)
    returned, gathered = lax.optimization_barrier((returned, gathered))
    returned = fold(GY, *thirds(returned))
    returned = fold(GZ, *thirds(returned))

    updated = pl.pallas_call(
        final_kernel,
        out_shape=jax.ShapeDtypeStruct((HARM, ATOMS, LANES), BF16),
        in_specs=[SMEM] + [VMEM] * 3,
        out_specs=VMEM,
        scratch_shapes=[pltpu.VMEM((ATOMS * 57, LANES), F32)],
        compiler_params=PARAMS,
    )(border_rows, feats, gathered, returned)
    return updated.transpose(1, 0, 2).reshape(features.shape)


def solution(mesh):
    fine = Mesh(mesh.devices.reshape(8, 4, 2, 4, 2), ("gx", "zh", "core", "x", "zl"))
    cell = ("gx", GY, GZ)
    plane = GY + GZ
    in_specs = (
        P(*cell, None, None, None),
        P(*cell, None),
        P(*cell, None),
        P(*cell, None),
        P(*cell, None),
        P(*cell),
        P(*cell, None),
        P(*cell, None),
        P(*cell, None, None),
        P(*cell),
        P(),
        P(plane, None),
        P(None, plane, None),
        P(None, plane, None),
    )
    out_specs = P(*cell, None, None, None)
    return jax.shard_map(shards, mesh=fine, in_specs=in_specs, out_specs=out_specs, check_vma=False)
```

```python
import functools

import jax
import jax.numpy as jnp
import numpy as np
from jax import lax
from jax.experimental import pallas as pl
from jax.experimental.pallas import tpu as pltpu
from jax.sharding import Mesh
from jax.sharding import PartitionSpec as P

LMAX = 6
HARM = (LMAX + 1) ** 2
JP = 56
KEPT = 29
KP = 32
EDGES = 128
ROTS = 256
ATOMS = 32
BOUND = 4
AROUND = 27 * BOUND
STEP = 32
PITCH = EDGES + 1
LANES = 128
BF16 = jnp.bfloat16
F32 = jnp.float32

SMEM = pl.BlockSpec(memory_space=pltpu.SMEM)
VMEM = pl.BlockSpec(memory_space=pltpu.VMEM)
HBM = pl.BlockSpec(memory_space=pltpu.HBM)
ANY = pl.BlockSpec(memory_space=pl.ANY)
PARAMS = pltpu.CompilerParams(vmem_limit_bytes=24 * 2**20)
WIDE = pltpu.CompilerParams(vmem_limit_bytes=58 * 2**20)

ROWS0, BLK0 = 16, 7
ROWS1, BLK1 = 24, 6
ROWS2, BLK2 = 20, 5
G0 = 4 * ROWS0 * BLK0
G1 = 4 * ROWS1 * BLK1
G2 = 4 * ROWS2 * BLK2
GROWS = G0 + G1 + G2


def kept_rows():
    listing = [d * d + d for d in range(LMAX + 1)]
    for shift in (1, -1, 2, -2):
        listing += [d * d + d + shift for d in range(abs(shift), LMAX + 1)]
    return listing


def slot_order():
    order = []
    for zh in range(4):
        for zl in range(2):
            for core in range(2):
                for x in range(4):
                    order.append(((zh * 2 + core) * 4 + x) * 2 + zl)
    return order


def spreads():
    order = slot_order()
    zero = np.zeros((2, 512, 512), np.float32)
    one = np.zeros((768, 768), np.float32)
    two = np.zeros((2, 768, 640), np.float32)
    for slot, shard in enumerate(order):
        half, local = divmod(slot, 32)
        for r in range(14):
            zero[half, shard * 14 + r - 384 * half, local * ROWS0 + r] = 1
        for r in range(12):
            if half == 0:
                one[shard * 12 + r, local * ROWS1 + r] = 1
                one[384 + shard * 12 + r, local * ROWS1 + 12 + r] = 1
        for r in range(10):
            two[half, shard * 10 + r - 256 * half, local * ROWS2 + r] = 1
            two[half, 384 + shard * 10 + r - 256 * half, local * ROWS2 + 10 + r] = 1
    return [jnp.asarray(m, BF16) for m in (zero, one, two)]


def tables_kernel(border_atoms, feats, x_out, border_out, tmp):
    for j in range(HARM):
        tmp[pl.ds(j * 33, ATOMS), :] = feats[j].astype(F32)
    tail = jnp.zeros((JP - HARM, LANES), F32)
    for a in range(ATOMS):
        rows = tmp[pl.ds(a, HARM, stride=33), :]
        x_out[a] = jnp.concatenate([rows, tail], axis=0).astype(BF16)
    for t in range(BOUND):
        border_out[t] = x_out[border_atoms[t]]


def share_kernel(zero, one, two, out):
    def columns(ref, b):
        return ref[..., b * LANES : (b + 1) * LANES].astype(F32)

    blank = jnp.zeros((2, LANES), F32)
    for b in range(BLK0):
        rows = jnp.concatenate([columns(zero, b), blank], axis=0)
        out[b * ROWS0 : (b + 1) * ROWS0, :] = rows.astype(BF16)
    start = ROWS0 * BLK0
    for b in range(BLK1):
        parts = columns(one, b)
        rows = jnp.concatenate([parts[:, 0, :], parts[:, 1, :]], axis=0)
        out[start + b * ROWS1 : start + (b + 1) * ROWS1, :] = rows.astype(BF16)
    start += ROWS1 * BLK1
    parts = [columns(two, b) for b in range(BLK2)]
    rows = jnp.concatenate([p[:, sign, :] for p in parts for sign in range(2)], axis=0)
    out[start:, :] = rows.astype(BF16)


def rotations_kernel(rotations, out, tmp):
    blank = jnp.zeros((LANES - HARM, ROTS), F32)
    for n, i in enumerate(kept_rows()):
        rows = jnp.concatenate([rotations[i].astype(F32), blank], axis=0)
        tmp[pl.ds(n, ROTS, stride=KP + 1), :] = rows.T
    for n in range(KEPT, KP):
        tmp[pl.ds(n, ROTS, stride=KP + 1), :] = jnp.zeros((ROTS, LANES), F32)
    for r in range(ROTS):
        out[r] = tmp[pl.ds(r * (KP + 1), KP), 0:JP].astype(BF16)


def blocks_of(count):
    return (count + (STEP - 1)) // STEP


def forward_kernel(sets, parts, *refs):
    counts, sources, picked = refs[0:sets], refs[sets : 2 * sets], refs[2 * sets : 3 * sets]
    refs = refs[3 * sets :]
    part_refs, table, spread_refs = refs[0:parts], refs[parts], refs[parts + 1 : parts + 4]
    outs, (tmp, x_ref, rot_ref, sp0, sp1, sp2, sems) = refs[parts + 5 : -7], refs[-7:]
    rows = x_ref.shape[0] // parts
    moves = [(part, x_ref.at[pl.ds(n * rows, rows)]) for n, part in enumerate(part_refs)]
    moves += [(table, rot_ref), *zip(spread_refs, (sp0, sp1, sp2), strict=True)]
    copies = [pltpu.make_async_copy(src, dst, sems.at[n]) for n, (src, dst) in enumerate(moves)]
    for copy in copies:
        copy.start()
    for copy in copies[:-3]:
        copy.wait()

    def spread(planes, matrix):
        return jnp.dot(jnp.concatenate(planes, axis=1), matrix, preferred_element_type=F32).astype(BF16)

    for i in range(sets):
        t0, t1, t2 = outs[3 * i : 3 * i + 3]

        def step(s, carry, i=i):
            for u in range(STEP):
                e = s * STEP + u
                rows = jnp.dot(rot_ref[picked[i][e]], x_ref[sources[i][e]], preferred_element_type=F32)
                tmp[i, pl.ds(e, KP, stride=PITCH), :] = rows
            return carry

        lax.fori_loop(0, blocks_of(counts[i][0]), step, 0)

        def plane(n, i=i):
            return tmp[i, pl.ds(n * PITCH, EDGES), :].astype(BF16)

        if i == 0:
            for copy in copies[-3:]:
                copy.wait()
        zero = [plane(n) for n in range(7)]
        t0[:, 0:512] = spread(zero[0:4], sp0[0])
        t0[:, 512:1024] = spread(zero[3:7], sp0[1])
        plus = [plane(7 + n) for n in range(6)]
        minus = [plane(13 + n) for n in range(6)]
        for h in range(2):
            p, q = plus[3 * h : 3 * h + 3], minus[3 * h : 3 * h + 3]
            t1[0, :, 768 * h : 768 * (h + 1)] = spread(p + [-m for m in q], sp1[...])
            t1[1, :, 768 * h : 768 * (h + 1)] = spread(q + p, sp1[...])
        plus = [plane(19 + n) for n in range(5)]
        minus = [plane(24 + n) for n in range(5)]
        for h in range(2):
            p, q = plus[2 * h : 2 * h + 3], minus[2 * h : 2 * h + 3]
            t2[0, :, 640 * h : 640 * (h + 1)] = spread(p + [-m for m in q], sp2[h])
            t2[1, :, 640 * h : 640 * (h + 1)] = spread(q + p, sp2[h])


def forward(counts, sources, picked, parts, table, sp, after):
    sets = len(counts)
    one = (
        jax.ShapeDtypeStruct((EDGES, 64 * ROWS0), BF16),
        jax.ShapeDtypeStruct((2, EDGES, 64 * ROWS1), BF16),
        jax.ShapeDtypeStruct((2, EDGES, 64 * ROWS2), BF16),
    )
    outs = pl.pallas_call(
        functools.partial(forward_kernel, sets, len(parts)),
        out_shape=one * sets,
        in_specs=[SMEM] * (3 * sets) + [HBM] * (len(parts) + 4) + [ANY],
        out_specs=(VMEM,) * (3 * sets),
        scratch_shapes=[
            pltpu.VMEM((sets, KP * PITCH, LANES), F32),
            pltpu.VMEM((len(parts) * parts[0].shape[0], JP, LANES), BF16),
            pltpu.VMEM((ROTS, KP, JP), BF16),
        ]
        + [pltpu.VMEM(m.shape, BF16) for m in sp]
        + [pltpu.SemaphoreType.DMA((len(parts) + 4,))],
        compiler_params=WIDE,
    )(*counts, *sources, *picked, *parts, table, *sp, after)
    return [outs[3 * i : 3 * i + 3] for i in range(sets)]


def back_kernel(sets, trash, finish, *refs):
    counts, picked, targets = refs[0:sets], refs[sets : 2 * sets], refs[2 * sets : 3 * sets]
    refs = refs[3 * sets :]
    sources = [refs[3 * i : 3 * i + 3] for i in range(sets)]
    table, gathered, _ = refs[3 * sets : 3 * sets + 3]
    refs = refs[3 * sets + 3 :]
    outs, (w0, w1, w2, t0, t1, t2, rot_ref, tmp, acc, sems) = refs[:-10], refs[-10:]
    moves = []
    start = 0
    for n, (weight, turned, size) in enumerate(((w0, t0, G0), (w1, t1, G1), (w2, t2, G2))):
        moves.append([(sources[i][n], turned.at[i]) for i in range(sets)])
        moves[-1].append((gathered.at[:, pl.ds(start, size), :], weight))
        start += size
    moves.append([(table, rot_ref)])
    copies = []
    for n, group in enumerate(moves):
        copies.append(
            [pltpu.make_async_copy(src, dst, sems.at[n, m]) for m, (src, dst) in enumerate(group)]
        )
        for copy in copies[-1]:
            copy.start()

    def arrived(n):
        for copy in copies[n]:
            copy.wait()

    acc[...] = jnp.zeros_like(acc)
    for i in range(sets):
        tmp[i, pl.ds(KEPT * PITCH, (KP - KEPT) * PITCH), :] = jnp.zeros(((KP - KEPT) * PITCH, LANES), F32)

    def mix(lhs, ref, rows, blocks, places):
        for b in range(0, blocks, 2):
            width = min(2, blocks - b)
            weight = [
                ref[:, (b + i) * rows : (b + i + 1) * rows, :].reshape(16 * rows, LANES) for i in range(width)
            ]
            weight = jnp.concatenate(weight, axis=1) if width == 2 else weight[0]
            result = jnp.dot(lhs, weight, preferred_element_type=F32)
            for n, (i, first) in enumerate(places):
                for w in range(width):
                    tmp[i, pl.ds((first + b + w) * PITCH, EDGES), :] = result[
                        n * EDGES : (n + 1) * EDGES, w * LANES : (w + 1) * LANES
                    ]

    arrived(0)
    mix(t0[...].reshape(sets * EDGES, 64 * ROWS0), w0, 4 * ROWS0, BLK0, [(i, 0) for i in range(sets)])
    for n, (lhs, ref, rows, blocks, first) in enumerate(((t1, w1, ROWS1, BLK1, 7), (t2, w2, ROWS2, BLK2, 19))):
        arrived(n + 1)
        mix(
            lhs[...].reshape(sets * 2 * EDGES, 64 * rows), ref, 4 * rows, blocks,
            [(i, first + sign * blocks) for i in range(sets) for sign in range(2)],
        )
    arrived(3)

    for i in range(sets):
        count = counts[i][0]

        def step(s, carry, i=i, count=count):
            for u in range(STEP):
                e = s * STEP + u
                rows = tmp[i, pl.ds(e, KP, stride=PITCH), :].astype(BF16)
                part = lax.dot_general(
                    rot_ref[picked[i][e]], rows, (((0,), (0,)), ((), ())), preferred_element_type=F32
                )
                acc[jnp.where(e < count, targets[i][e], trash)] += part
            return carry

        lax.fori_loop(0, blocks_of(count), step, 0)
    finish(acc, *outs)


def store_returned(acc, first, middle, last):
    first[...] = acc[0:36].astype(BF16)
    middle[...] = acc[36:72]
    last[...] = acc[72:108].astype(BF16)


def store_gathered(acc, out):
    out[...] = acc[0:ATOMS]


def back(counts, picked, targets, turned, table, gathered, after, rows, trash, finish, out_shape):
    sets = len(counts)
    return pl.pallas_call(
        functools.partial(back_kernel, sets, trash, finish),
        out_shape=out_shape,
        in_specs=[SMEM] * (3 * sets) + [HBM] * (3 * sets + 2) + [ANY],
        out_specs=jax.tree.map(lambda _: VMEM, out_shape),
        scratch_shapes=[
            pltpu.VMEM((16, G0, LANES), BF16),
            pltpu.VMEM((16, G1, LANES), BF16),
            pltpu.VMEM((16, G2, LANES), BF16),
            pltpu.VMEM((sets, EDGES, 64 * ROWS0), BF16),
            pltpu.VMEM((sets, 2, EDGES, 64 * ROWS1), BF16),
            pltpu.VMEM((sets, 2, EDGES, 64 * ROWS2), BF16),
            pltpu.VMEM((ROTS, KP, JP), BF16),
            pltpu.VMEM((sets, KP * PITCH, LANES), F32),
            pltpu.VMEM((rows, JP, LANES), F32),
            pltpu.SemaphoreType.DMA((4, sets + 1)),
        ],
        compiler_params=WIDE,
    )(*counts, *picked, *targets, *[t for one in turned for t in one], table, gathered, after)


def final_kernel(border_atoms, feats, gathered, returned, out, acc):
    for a in range(ATOMS):
        acc[pl.ds(a * 57, JP), :] = gathered[a]
    for t in range(BOUND):
        acc[pl.ds(border_atoms[t] * 57, JP), :] += returned[t]
    for j in range(HARM):
        total = acc[pl.ds(j, ATOMS, stride=57), :]
        out[j] = (feats[j].astype(F32) + 0.25 * total).astype(BF16)


def swap(axis, block, odd):
    count = lax.axis_size(axis)
    return lax.ppermute(block, axis, [(i, (i + (1 if (i + odd) % 2 == 0 else -1)) % count) for i in range(count)])


def exchange(axis, first, last):
    last = swap(axis, last, 1)
    if axis == GY:
        both = lax.all_gather(first, "core", axis=0, tiled=False)
        return jnp.where(lax.axis_index("core") == 0, both[1], both[0]), last
    return swap(axis, first, 0), last


def widen(axis, block):
    first, last = exchange(axis, block, block)
    return jnp.concatenate([first, block, last], axis=0)


def fold(axis, first, middle, last):
    first, last = exchange(axis, first, last)
    return middle + first.astype(F32) + last.astype(F32)


def thirds(block):
    third = block.shape[0] // 3
    return block[:third].astype(BF16), block[third : 2 * third], block[2 * third :].astype(BF16)


GX, GY, GZ = "gx", ("zh", "core"), ("x", "zl")


def shards(
    features,
    border_atoms,
    inner_source,
    inner_target,
    inner_rotation,
    inner_count,
    cross_source,
    cross_target,
    cross_rotation,
    cross_count,
    rotations,
    order_zero,
    order_one,
    order_two,
):
    share = pl.pallas_call(
        share_kernel,
        out_shape=jax.ShapeDtypeStruct((ROWS0 * BLK0 + ROWS1 * BLK1 + ROWS2 * BLK2, LANES), BF16),
        in_specs=[VMEM] * 3,
        out_specs=VMEM,
        compiler_params=WIDE,
    )(order_zero, order_one.transpose(1, 0, 2), order_two.transpose(1, 0, 2))
    four = lax.all_gather(share, "x", axis=0, tiled=False)
    pieces = []
    start = 0
    for rows, blocks in ((ROWS0, BLK0), (ROWS1, BLK1), (ROWS2, BLK2)):
        piece = four[:, start : start + rows * blocks].reshape(4, blocks, rows, LANES)
        pieces.append(piece.transpose(1, 0, 2, 3).reshape(blocks * 4 * rows, LANES))
        start += rows * blocks
    gathered_weights = lax.all_gather(jnp.concatenate(pieces, axis=0), ("zh", "zl", "core"), axis=0, tiled=False)

    feats = features[0, 0, 0].transpose(1, 0, 2)
    border_rows = border_atoms[0, 0, 0]
    x, border = pl.pallas_call(
        tables_kernel,
        out_shape=(
            jax.ShapeDtypeStruct((ATOMS, JP, LANES), BF16),
            jax.ShapeDtypeStruct((BOUND, JP, LANES), BF16),
        ),
        in_specs=[SMEM, VMEM],
        out_specs=(VMEM, VMEM),
        scratch_shapes=[pltpu.VMEM((HARM * 33, LANES), F32)],
        compiler_params=PARAMS,
    )(border_rows, feats)

    table = pl.pallas_call(
        rotations_kernel,
        out_shape=jax.ShapeDtypeStruct((ROTS, KP, JP), BF16),
        in_specs=[VMEM],
        out_specs=VMEM,
        scratch_shapes=[pltpu.VMEM((ROTS * (KP + 1), LANES), F32)],
        compiler_params=pltpu.CompilerParams(vmem_limit_bytes=12 * 2**20),
    )(rotations)

    sp = spreads()
    count_in, count_x = inner_count.reshape(1), cross_count.reshape(1)
    source_in, target_in, rot_in = inner_source[0, 0, 0], inner_target[0, 0, 0], inner_rotation[0, 0, 0]
    far_rows, target_x = cross_source[0, 0, 0], cross_target[0, 0, 0]
    rot_inward, rot_outward = cross_rotation[0, 0, 0, 0], cross_rotation[0, 0, 0, 1]
    def place(axis, offset):
        return jnp.where(lax.axis_index(axis) % 2 == 1, offset, 2 - offset)

    slot, atom = far_rows // BOUND, far_rows % BOUND
    far_rows = (place(GX, slot // 9) * 3 + place(GY, slot // 3 % 3)) * 3 + place(GZ, slot % 3)
    far_rows = far_rows * BOUND + atom

    near = widen(GY, widen(GZ, border))
    near_first, near_last = exchange(GX, near, near)
    turned_out, turned_in = forward(
        [count_x, count_in], [target_x, source_in], [rot_outward, rot_in], [x], table, sp, near
    )
    [turned_x] = forward(
        [count_x], [far_rows], [rot_inward], [near_first, near, near_last], table, sp, turned_in[0]
    )

    face = (36, JP, LANES)
    first, middle, last = back(
        [count_x], [rot_outward], [far_rows], [turned_out], table, gathered_weights, turned_x[0], 112, AROUND,
        store_returned,
        (jax.ShapeDtypeStruct(face, BF16), jax.ShapeDtypeStruct(face, F32), jax.ShapeDtypeStruct(face, BF16)),
    )
    gathered = back(
        [count_in, count_x], [rot_in, rot_inward], [target_in, target_x], [turned_in, turned_x], table,
        gathered_weights, first, 40, ATOMS, store_gathered, jax.ShapeDtypeStruct((ATOMS, JP, LANES), F32),
    )
    returned = fold(GX, first, middle, last)
    returned, gathered = lax.optimization_barrier((returned, gathered))
    returned = fold(GY, *thirds(returned))
    returned = fold(GZ, *thirds(returned))

    updated = pl.pallas_call(
        final_kernel,
        out_shape=jax.ShapeDtypeStruct((HARM, ATOMS, LANES), BF16),
        in_specs=[SMEM] + [VMEM] * 3,
        out_specs=VMEM,
        scratch_shapes=[pltpu.VMEM((ATOMS * 57, LANES), F32)],
        compiler_params=PARAMS,
    )(border_rows, feats, gathered, returned)
    return updated.transpose(1, 0, 2).reshape(features.shape)


def solution(mesh):
    fine = Mesh(mesh.devices.reshape(8, 4, 2, 4, 2), ("gx", "zh", "core", "x", "zl"))
    cell = ("gx", GY, GZ)
    plane = GY + GZ
    in_specs = (
        P(*cell, None, None, None),
        P(*cell, None),
        P(*cell, None),
        P(*cell, None),
        P(*cell, None),
        P(*cell),
        P(*cell, None),
        P(*cell, None),
        P(*cell, None, None),
        P(*cell),
        P(),
        P(plane, None),
        P(None, plane, None),
        P(None, plane, None),
    )
    out_specs = P(*cell, None, None, None)
    return jax.shard_map(shards, mesh=fine, in_specs=in_specs, out_specs=out_specs, check_vma=False)
```

```python
import functools

import jax
import jax.numpy as jnp
import numpy as np
from jax import lax
from jax.experimental import pallas as pl
from jax.experimental.pallas import tpu as pltpu
from jax.sharding import Mesh
from jax.sharding import PartitionSpec as P

LMAX = 6
HARM = (LMAX + 1) ** 2
JP = 56
KEPT = 29
KP = 32
EDGES = 128
ROTS = 256
ATOMS = 32
BOUND = 4
AROUND = 27 * BOUND
STEP = 64
PITCH = EDGES + 1
LANES = 128
BF16 = jnp.bfloat16
F32 = jnp.float32

SMEM = pl.BlockSpec(memory_space=pltpu.SMEM)
VMEM = pl.BlockSpec(memory_space=pltpu.VMEM)
HBM = pl.BlockSpec(memory_space=pltpu.HBM)
ANY = pl.BlockSpec(memory_space=pl.ANY)
PARAMS = pltpu.CompilerParams(vmem_limit_bytes=24 * 2**20)
WIDE = pltpu.CompilerParams(vmem_limit_bytes=58 * 2**20)

ROWS0, BLK0 = 16, 7
ROWS1, BLK1 = 24, 6
ROWS2, BLK2 = 20, 5
G0 = 4 * ROWS0 * BLK0
G1 = 4 * ROWS1 * BLK1
G2 = 4 * ROWS2 * BLK2
GROWS = G0 + G1 + G2


def kept_rows():
    listing = [d * d + d for d in range(LMAX + 1)]
    for shift in (1, -1, 2, -2):
        listing += [d * d + d + shift for d in range(abs(shift), LMAX + 1)]
    return listing


def slot_order():
    order = []
    for zh in range(4):
        for zl in range(2):
            for core in range(2):
                for x in range(4):
                    order.append(((zh * 2 + core) * 4 + x) * 2 + zl)
    return order


def spreads():
    order = slot_order()
    zero = np.zeros((2, 512, 512), np.float32)
    one = np.zeros((768, 768), np.float32)
    two = np.zeros((2, 768, 640), np.float32)
    for slot, shard in enumerate(order):
        half, local = divmod(slot, 32)
        for r in range(14):
            zero[half, shard * 14 + r - 384 * half, local * ROWS0 + r] = 1
        for r in range(12):
            if half == 0:
                one[shard * 12 + r, local * ROWS1 + r] = 1
                one[384 + shard * 12 + r, local * ROWS1 + 12 + r] = 1
        for r in range(10):
            two[half, shard * 10 + r - 256 * half, local * ROWS2 + r] = 1
            two[half, 384 + shard * 10 + r - 256 * half, local * ROWS2 + 10 + r] = 1
    return [jnp.asarray(m, BF16) for m in (zero, one, two)]


def tables_kernel(border_atoms, feats, x_out, border_out, tmp):
    for j in range(HARM):
        tmp[pl.ds(j * 33, ATOMS), :] = feats[j].astype(F32)
    tail = jnp.zeros((JP - HARM, LANES), F32)
    for a in range(ATOMS):
        rows = tmp[pl.ds(a, HARM, stride=33), :]
        x_out[a] = jnp.concatenate([rows, tail], axis=0).astype(BF16)
    for t in range(BOUND):
        border_out[t] = x_out[border_atoms[t]]


def share_kernel(zero, one, two, out):
    def columns(ref, b):
        return ref[..., b * LANES : (b + 1) * LANES].astype(F32)

    blank = jnp.zeros((2, LANES), F32)
    for b in range(BLK0):
        rows = jnp.concatenate([columns(zero, b), blank], axis=0)
        out[b * ROWS0 : (b + 1) * ROWS0, :] = rows.astype(BF16)
    start = ROWS0 * BLK0
    for b in range(BLK1):
        parts = columns(one, b)
        rows = jnp.concatenate([parts[:, 0, :], parts[:, 1, :]], axis=0)
        out[start + b * ROWS1 : start + (b + 1) * ROWS1, :] = rows.astype(BF16)
    start += ROWS1 * BLK1
    parts = [columns(two, b) for b in range(BLK2)]
    rows = jnp.concatenate([p[:, sign, :] for p in parts for sign in range(2)], axis=0)
    out[start:, :] = rows.astype(BF16)


def rotations_kernel(rotations, out, tmp):
    blank = jnp.zeros((LANES - HARM, ROTS), F32)
    for n, i in enumerate(kept_rows()):
        rows = jnp.concatenate([rotations[i].astype(F32), blank], axis=0)
        tmp[pl.ds(n, ROTS, stride=KP + 1), :] = rows.T
    for n in range(KEPT, KP):
        tmp[pl.ds(n, ROTS, stride=KP + 1), :] = jnp.zeros((ROTS, LANES), F32)
    for r in range(ROTS):
        out[r] = tmp[pl.ds(r * (KP + 1), KP), 0:JP].astype(BF16)


def blocks_of(count):
    return (count + (STEP - 1)) // STEP


def forward_kernel(sets, parts, *refs):
    counts, sources, picked = refs[0:sets], refs[sets : 2 * sets], refs[2 * sets : 3 * sets]
    refs = refs[3 * sets :]
    part_refs, table, spread_refs = refs[0:parts], refs[parts], refs[parts + 1 : parts + 4]
    outs, (tmp, x_ref, rot_ref, sp0, sp1, sp2, sems) = refs[parts + 5 : -7], refs[-7:]
    rows = x_ref.shape[0] // parts
    moves = [(part, x_ref.at[pl.ds(n * rows, rows)]) for n, part in enumerate(part_refs)]
    moves += [(table, rot_ref), *zip(spread_refs, (sp0, sp1, sp2), strict=True)]
    copies = [pltpu.make_async_copy(src, dst, sems.at[n]) for n, (src, dst) in enumerate(moves)]
    for copy in copies:
        copy.start()
    for copy in copies[:-3]:
        copy.wait()

    def spread(planes, matrix):
        return jnp.dot(jnp.concatenate(planes, axis=1), matrix, preferred_element_type=F32).astype(BF16)

    for i in range(sets):
        t0, t1, t2 = outs[3 * i : 3 * i + 3]

        def step(s, carry, i=i):
            for u in range(STEP):
                e = s * STEP + u
                rows = jnp.dot(rot_ref[picked[i][e]], x_ref[sources[i][e]], preferred_element_type=F32)
                tmp[i, pl.ds(e, KP, stride=PITCH), :] = rows
            return carry

        lax.fori_loop(0, blocks_of(counts[i][0]), step, 0)

        def plane(n, i=i):
            return tmp[i, pl.ds(n * PITCH, EDGES), :].astype(BF16)

        if i == 0:
            for copy in copies[-3:]:
                copy.wait()
        zero = [plane(n) for n in range(7)]
        t0[:, 0:512] = spread(zero[0:4], sp0[0])
        t0[:, 512:1024] = spread(zero[3:7], sp0[1])
        plus = [plane(7 + n) for n in range(6)]
        minus = [plane(13 + n) for n in range(6)]
        for h in range(2):
            p, q = plus[3 * h : 3 * h + 3], minus[3 * h : 3 * h + 3]
            t1[0, :, 768 * h : 768 * (h + 1)] = spread(p + [-m for m in q], sp1[...])
            t1[1, :, 768 * h : 768 * (h + 1)] = spread(q + p, sp1[...])
        plus = [plane(19 + n) for n in range(5)]
        minus = [plane(24 + n) for n in range(5)]
        for h in range(2):
            p, q = plus[2 * h : 2 * h + 3], minus[2 * h : 2 * h + 3]
            t2[0, :, 640 * h : 640 * (h + 1)] = spread(p + [-m for m in q], sp2[h])
            t2[1, :, 640 * h : 640 * (h + 1)] = spread(q + p, sp2[h])


def forward(counts, sources, picked, parts, table, sp, after):
    sets = len(counts)
    one = (
        jax.ShapeDtypeStruct((EDGES, 64 * ROWS0), BF16),
        jax.ShapeDtypeStruct((2, EDGES, 64 * ROWS1), BF16),
        jax.ShapeDtypeStruct((2, EDGES, 64 * ROWS2), BF16),
    )
    outs = pl.pallas_call(
        functools.partial(forward_kernel, sets, len(parts)),
        out_shape=one * sets,
        in_specs=[SMEM] * (3 * sets) + [HBM] * (len(parts) + 4) + [ANY],
        out_specs=(VMEM,) * (3 * sets),
        scratch_shapes=[
            pltpu.VMEM((sets, KP * PITCH, LANES), F32),
            pltpu.VMEM((len(parts) * parts[0].shape[0], JP, LANES), BF16),
            pltpu.VMEM((ROTS, KP, JP), BF16),
        ]
        + [pltpu.VMEM(m.shape, BF16) for m in sp]
        + [pltpu.SemaphoreType.DMA((len(parts) + 4,))],
        compiler_params=WIDE,
    )(*counts, *sources, *picked, *parts, table, *sp, after)
    return [outs[3 * i : 3 * i + 3] for i in range(sets)]


def back_kernel(sets, trash, finish, *refs):
    counts, picked, targets = refs[0:sets], refs[sets : 2 * sets], refs[2 * sets : 3 * sets]
    refs = refs[3 * sets :]
    sources = [refs[3 * i : 3 * i + 3] for i in range(sets)]
    table, gathered, _ = refs[3 * sets : 3 * sets + 3]
    refs = refs[3 * sets + 3 :]
    outs, (w0, w1, w2, t0, t1, t2, rot_ref, tmp, acc, sems) = refs[:-10], refs[-10:]
    moves = []
    start = 0
    for n, (weight, turned, size) in enumerate(((w0, t0, G0), (w1, t1, G1), (w2, t2, G2))):
        moves.append([(sources[i][n], turned.at[i]) for i in range(sets)])
        moves[-1].append((gathered.at[:, pl.ds(start, size), :], weight))
        start += size
    moves.append([(table, rot_ref)])
    copies = []
    for n, group in enumerate(moves):
        copies.append(
            [pltpu.make_async_copy(src, dst, sems.at[n, m]) for m, (src, dst) in enumerate(group)]
        )
        for copy in copies[-1]:
            copy.start()

    def arrived(n):
        for copy in copies[n]:
            copy.wait()

    acc[...] = jnp.zeros_like(acc)
    for i in range(sets):
        tmp[i, pl.ds(KEPT * PITCH, (KP - KEPT) * PITCH), :] = jnp.zeros(((KP - KEPT) * PITCH, LANES), F32)

    def mix(lhs, ref, rows, blocks, places):
        for b in range(0, blocks, 2):
            width = min(2, blocks - b)
            weight = [
                ref[:, (b + i) * rows : (b + i + 1) * rows, :].reshape(16 * rows, LANES) for i in range(width)
            ]
            weight = jnp.concatenate(weight, axis=1) if width == 2 else weight[0]
            result = jnp.dot(lhs, weight, preferred_element_type=F32)
            for n, (i, first) in enumerate(places):
                for w in range(width):
                    tmp[i, pl.ds((first + b + w) * PITCH, EDGES), :] = result[
                        n * EDGES : (n + 1) * EDGES, w * LANES : (w + 1) * LANES
                    ]

    arrived(0)
    mix(t0[...].reshape(sets * EDGES, 64 * ROWS0), w0, 4 * ROWS0, BLK0, [(i, 0) for i in range(sets)])
    for n, (lhs, ref, rows, blocks, first) in enumerate(((t1, w1, ROWS1, BLK1, 7), (t2, w2, ROWS2, BLK2, 19))):
        arrived(n + 1)
        mix(
            lhs[...].reshape(sets * 2 * EDGES, 64 * rows), ref, 4 * rows, blocks,
            [(i, first + sign * blocks) for i in range(sets) for sign in range(2)],
        )
    arrived(3)

    for i in range(sets):
        count = counts[i][0]

        def step(s, carry, i=i, count=count):
            for u in range(STEP):
                e = s * STEP + u
                rows = tmp[i, pl.ds(e, KP, stride=PITCH), :].astype(BF16)
                part = lax.dot_general(
                    rot_ref[picked[i][e]], rows, (((0,), (0,)), ((), ())), preferred_element_type=F32
                )
                acc[jnp.where(e < count, targets[i][e], trash)] += part
            return carry

        lax.fori_loop(0, blocks_of(count), step, 0)
    finish(acc, *outs)


def store_returned(acc, first, middle, last):
    first[...] = acc[0:36].astype(BF16)
    middle[...] = acc[36:72]
    last[...] = acc[72:108].astype(BF16)


def store_gathered(acc, out):
    out[...] = acc[0:ATOMS]


def back(counts, picked, targets, turned, table, gathered, after, rows, trash, finish, out_shape):
    sets = len(counts)
    return pl.pallas_call(
        functools.partial(back_kernel, sets, trash, finish),
        out_shape=out_shape,
        in_specs=[SMEM] * (3 * sets) + [HBM] * (3 * sets + 2) + [ANY],
        out_specs=jax.tree.map(lambda _: VMEM, out_shape),
        scratch_shapes=[
            pltpu.VMEM((16, G0, LANES), BF16),
            pltpu.VMEM((16, G1, LANES), BF16),
            pltpu.VMEM((16, G2, LANES), BF16),
            pltpu.VMEM((sets, EDGES, 64 * ROWS0), BF16),
            pltpu.VMEM((sets, 2, EDGES, 64 * ROWS1), BF16),
            pltpu.VMEM((sets, 2, EDGES, 64 * ROWS2), BF16),
            pltpu.VMEM((ROTS, KP, JP), BF16),
            pltpu.VMEM((sets, KP * PITCH, LANES), F32),
            pltpu.VMEM((rows, JP, LANES), F32),
            pltpu.SemaphoreType.DMA((4, sets + 1)),
        ],
        compiler_params=WIDE,
    )(*counts, *picked, *targets, *[t for one in turned for t in one], table, gathered, after)


def final_kernel(border_atoms, feats, gathered, returned, out, acc):
    for a in range(ATOMS):
        acc[pl.ds(a * 57, JP), :] = gathered[a]
    for t in range(BOUND):
        acc[pl.ds(border_atoms[t] * 57, JP), :] += returned[t]
    for j in range(HARM):
        total = acc[pl.ds(j, ATOMS, stride=57), :]
        out[j] = (feats[j].astype(F32) + 0.25 * total).astype(BF16)


def swap(axis, block, odd):
    count = lax.axis_size(axis)
    return lax.ppermute(block, axis, [(i, (i + (1 if (i + odd) % 2 == 0 else -1)) % count) for i in range(count)])


def exchange(axis, first, last):
    last = swap(axis, last, 1)
    if axis == GY:
        both = lax.all_gather(first, "core", axis=0, tiled=False)
        return jnp.where(lax.axis_index("core") == 0, both[1], both[0]), last
    return swap(axis, first, 0), last


def widen(axis, block):
    first, last = exchange(axis, block, block)
    return jnp.concatenate([first, block, last], axis=0)


def fold(axis, first, middle, last):
    first, last = exchange(axis, first, last)
    return middle + first.astype(F32) + last.astype(F32)


def thirds(block):
    third = block.shape[0] // 3
    return block[:third].astype(BF16), block[third : 2 * third], block[2 * third :].astype(BF16)


GX, GY, GZ = "gx", ("zh", "core"), ("x", "zl")


def shards(
    features,
    border_atoms,
    inner_source,
    inner_target,
    inner_rotation,
    inner_count,
    cross_source,
    cross_target,
    cross_rotation,
    cross_count,
    rotations,
    order_zero,
    order_one,
    order_two,
):
    share = pl.pallas_call(
        share_kernel,
        out_shape=jax.ShapeDtypeStruct((ROWS0 * BLK0 + ROWS1 * BLK1 + ROWS2 * BLK2, LANES), BF16),
        in_specs=[VMEM] * 3,
        out_specs=VMEM,
        compiler_params=WIDE,
    )(order_zero, order_one.transpose(1, 0, 2), order_two.transpose(1, 0, 2))
    four = lax.all_gather(share, "x", axis=0, tiled=False)
    pieces = []
    start = 0
    for rows, blocks in ((ROWS0, BLK0), (ROWS1, BLK1), (ROWS2, BLK2)):
        piece = four[:, start : start + rows * blocks].reshape(4, blocks, rows, LANES)
        pieces.append(piece.transpose(1, 0, 2, 3).reshape(blocks * 4 * rows, LANES))
        start += rows * blocks
    gathered_weights = lax.all_gather(jnp.concatenate(pieces, axis=0), ("zh", "zl", "core"), axis=0, tiled=False)

    feats = features[0, 0, 0].transpose(1, 0, 2)
    border_rows = border_atoms[0, 0, 0]
    x, border = pl.pallas_call(
        tables_kernel,
        out_shape=(
            jax.ShapeDtypeStruct((ATOMS, JP, LANES), BF16),
            jax.ShapeDtypeStruct((BOUND, JP, LANES), BF16),
        ),
        in_specs=[SMEM, VMEM],
        out_specs=(VMEM, VMEM),
        scratch_shapes=[pltpu.VMEM((HARM * 33, LANES), F32)],
        compiler_params=PARAMS,
    )(border_rows, feats)

    table = pl.pallas_call(
        rotations_kernel,
        out_shape=jax.ShapeDtypeStruct((ROTS, KP, JP), BF16),
        in_specs=[VMEM],
        out_specs=VMEM,
        scratch_shapes=[pltpu.VMEM((ROTS * (KP + 1), LANES), F32)],
        compiler_params=pltpu.CompilerParams(vmem_limit_bytes=12 * 2**20),
    )(rotations)

    sp = spreads()
    count_in, count_x = inner_count.reshape(1), cross_count.reshape(1)
    source_in, target_in, rot_in = inner_source[0, 0, 0], inner_target[0, 0, 0], inner_rotation[0, 0, 0]
    far_rows, target_x = cross_source[0, 0, 0], cross_target[0, 0, 0]
    rot_inward, rot_outward = cross_rotation[0, 0, 0, 0], cross_rotation[0, 0, 0, 1]
    def place(axis, offset):
        return jnp.where(lax.axis_index(axis) % 2 == 1, offset, 2 - offset)

    slot, atom = far_rows // BOUND, far_rows % BOUND
    far_rows = (place(GX, slot // 9) * 3 + place(GY, slot // 3 % 3)) * 3 + place(GZ, slot % 3)
    far_rows = far_rows * BOUND + atom

    near = widen(GY, widen(GZ, border))
    near, table = lax.optimization_barrier((near, table))
    near_first, near_last = exchange(GX, near, near)
    turned_out, turned_in = forward(
        [count_x, count_in], [target_x, source_in], [rot_outward, rot_in], [x], table, sp, near
    )
    [turned_x] = forward(
        [count_x], [far_rows], [rot_inward], [near_first, near, near_last], table, sp, turned_in[0]
    )

    face = (36, JP, LANES)
    first, middle, last = back(
        [count_x], [rot_outward], [far_rows], [turned_out], table, gathered_weights, turned_x[0], 112, AROUND,
        store_returned,
        (jax.ShapeDtypeStruct(face, BF16), jax.ShapeDtypeStruct(face, F32), jax.ShapeDtypeStruct(face, BF16)),
    )
    gathered = back(
        [count_in, count_x], [rot_in, rot_inward], [target_in, target_x], [turned_in, turned_x], table,
        gathered_weights, first, 40, ATOMS, store_gathered, jax.ShapeDtypeStruct((ATOMS, JP, LANES), F32),
    )
    returned = fold(GX, first, middle, last)
    returned, gathered = lax.optimization_barrier((returned, gathered))
    returned = fold(GY, *thirds(returned))
    returned = fold(GZ, *thirds(returned))

    updated = pl.pallas_call(
        final_kernel,
        out_shape=jax.ShapeDtypeStruct((HARM, ATOMS, LANES), BF16),
        in_specs=[SMEM] + [VMEM] * 3,
        out_specs=VMEM,
        scratch_shapes=[pltpu.VMEM((ATOMS * 57, LANES), F32)],
        compiler_params=PARAMS,
    )(border_rows, feats, gathered, returned)
    return updated.transpose(1, 0, 2).reshape(features.shape)


def solution(mesh):
    fine = Mesh(mesh.devices.reshape(8, 4, 2, 4, 2), ("gx", "zh", "core", "x", "zl"))
    cell = ("gx", GY, GZ)
    plane = GY + GZ
    in_specs = (
        P(*cell, None, None, None),
        P(*cell, None),
        P(*cell, None),
        P(*cell, None),
        P(*cell, None),
        P(*cell),
        P(*cell, None),
        P(*cell, None),
        P(*cell, None, None),
        P(*cell),
        P(),
        P(plane, None),
        P(None, plane, None),
        P(None, plane, None),
    )
    out_specs = P(*cell, None, None, None)
    return jax.shard_map(shards, mesh=fine, in_specs=in_specs, out_specs=out_specs, check_vma=False)
```

```python
import functools

import jax
import jax.numpy as jnp
import numpy as np
from jax import lax
from jax.experimental import pallas as pl
from jax.experimental.pallas import tpu as pltpu
from jax.sharding import Mesh
from jax.sharding import PartitionSpec as P

LMAX = 6
HARM = (LMAX + 1) ** 2
JP = 56
KEPT = 29
KP = 32
EDGES = 128
ROTS = 256
ATOMS = 32
BOUND = 4
AROUND = 27 * BOUND
STEP = 64
PITCH = EDGES + 1
LANES = 128
BF16 = jnp.bfloat16
F32 = jnp.float32

SMEM = pl.BlockSpec(memory_space=pltpu.SMEM)
VMEM = pl.BlockSpec(memory_space=pltpu.VMEM)
HBM = pl.BlockSpec(memory_space=pltpu.HBM)
ANY = pl.BlockSpec(memory_space=pl.ANY)
PARAMS = pltpu.CompilerParams(vmem_limit_bytes=24 * 2**20)
WIDE = pltpu.CompilerParams(vmem_limit_bytes=58 * 2**20)

ROWS0, BLK0 = 16, 7
ROWS1, BLK1 = 24, 6
ROWS2, BLK2 = 20, 5
G0 = 4 * ROWS0 * BLK0
G1 = 4 * ROWS1 * BLK1
G2 = 4 * ROWS2 * BLK2
GROWS = G0 + G1 + G2


def kept_rows():
    listing = [d * d + d for d in range(LMAX + 1)]
    for shift in (1, -1, 2, -2):
        listing += [d * d + d + shift for d in range(abs(shift), LMAX + 1)]
    return listing


def slot_order():
    order = []
    for zh in range(4):
        for zl in range(2):
            for core in range(2):
                for x in range(4):
                    order.append(((zh * 2 + core) * 4 + x) * 2 + zl)
    return order


def spreads():
    order = slot_order()
    zero = np.zeros((2, 512, 512), np.float32)
    one = np.zeros((768, 768), np.float32)
    two = np.zeros((2, 768, 640), np.float32)
    for slot, shard in enumerate(order):
        half, local = divmod(slot, 32)
        for r in range(14):
            zero[half, shard * 14 + r - 384 * half, local * ROWS0 + r] = 1
        for r in range(12):
            if half == 0:
                one[shard * 12 + r, local * ROWS1 + r] = 1
                one[384 + shard * 12 + r, local * ROWS1 + 12 + r] = 1
        for r in range(10):
            two[half, shard * 10 + r - 256 * half, local * ROWS2 + r] = 1
            two[half, 384 + shard * 10 + r - 256 * half, local * ROWS2 + 10 + r] = 1
    return [jnp.asarray(m, BF16) for m in (zero, one, two)]


def tables_kernel(border_atoms, feats, x_out, border_out, tmp):
    for j in range(HARM):
        tmp[pl.ds(j * 33, ATOMS), :] = feats[j].astype(F32)
    tail = jnp.zeros((JP - HARM, LANES), F32)
    for a in range(ATOMS):
        rows = tmp[pl.ds(a, HARM, stride=33), :]
        x_out[a] = jnp.concatenate([rows, tail], axis=0).astype(BF16)
    for t in range(BOUND):
        border_out[t] = x_out[border_atoms[t]]


def share_kernel(zero, one, two, out):
    def columns(ref, b):
        return ref[..., b * LANES : (b + 1) * LANES].astype(F32)

    blank = jnp.zeros((2, LANES), F32)
    for b in range(BLK0):
        rows = jnp.concatenate([columns(zero, b), blank], axis=0)
        out[b * ROWS0 : (b + 1) * ROWS0, :] = rows.astype(BF16)
    start = ROWS0 * BLK0
    for b in range(BLK1):
        parts = columns(one, b)
        rows = jnp.concatenate([parts[:, 0, :], parts[:, 1, :]], axis=0)
        out[start + b * ROWS1 : start + (b + 1) * ROWS1, :] = rows.astype(BF16)
    start += ROWS1 * BLK1
    parts = [columns(two, b) for b in range(BLK2)]
    rows = jnp.concatenate([p[:, sign, :] for p in parts for sign in range(2)], axis=0)
    out[start:, :] = rows.astype(BF16)


def rotations_kernel(rotations, out, tmp):
    blank = jnp.zeros((LANES - HARM, ROTS), F32)
    for n, i in enumerate(kept_rows()):
        rows = jnp.concatenate([rotations[i].astype(F32), blank], axis=0)
        tmp[pl.ds(n, ROTS, stride=KP + 1), :] = rows.T
    for n in range(KEPT, KP):
        tmp[pl.ds(n, ROTS, stride=KP + 1), :] = jnp.zeros((ROTS, LANES), F32)
    for r in range(ROTS):
        out[r] = tmp[pl.ds(r * (KP + 1), KP), 0:JP].astype(BF16)


def blocks_of(count):
    return (count + (STEP - 1)) // STEP


def forward_kernel(sets, parts, *refs):
    counts, sources, picked = refs[0:sets], refs[sets : 2 * sets], refs[2 * sets : 3 * sets]
    refs = refs[3 * sets :]
    part_refs, table, spread_refs = refs[0:parts], refs[parts], refs[parts + 1 : parts + 4]
    outs, (tmp, x_ref, rot_ref, sp0, sp1, sp2, sems) = refs[parts + 5 : -7], refs[-7:]
    rows = x_ref.shape[0] // parts
    moves = [(part, x_ref.at[pl.ds(n * rows, rows)]) for n, part in enumerate(part_refs)]
    moves += [(table, rot_ref), *zip(spread_refs, (sp0, sp1, sp2), strict=True)]
    copies = [pltpu.make_async_copy(src, dst, sems.at[n]) for n, (src, dst) in enumerate(moves)]
    for copy in copies:
        copy.start()
    for copy in copies[:-3]:
        copy.wait()

    def spread(planes, matrix):
        return jnp.dot(jnp.concatenate(planes, axis=1), matrix, preferred_element_type=F32).astype(BF16)

    for i in range(sets):
        t0, t1, t2 = outs[3 * i : 3 * i + 3]

        def step(s, carry, i=i):
            for u in range(STEP):
                e = s * STEP + u
                rows = jnp.dot(rot_ref[picked[i][e]], x_ref[sources[i][e]], preferred_element_type=F32)
                tmp[i, pl.ds(e, KP, stride=PITCH), :] = rows
            return carry

        lax.fori_loop(0, blocks_of(counts[i][0]), step, 0)

        def plane(n, i=i):
            return tmp[i, pl.ds(n * PITCH, EDGES), :].astype(BF16)

        if i == 0:
            for copy in copies[-3:]:
                copy.wait()
        zero = [plane(n) for n in range(7)]
        t0[:, 0:512] = spread(zero[0:4], sp0[0])
        t0[:, 512:1024] = spread(zero[3:7], sp0[1])
        plus = [plane(7 + n) for n in range(6)]
        minus = [plane(13 + n) for n in range(6)]
        for h in range(2):
            p, q = plus[3 * h : 3 * h + 3], minus[3 * h : 3 * h + 3]
            t1[0, :, 768 * h : 768 * (h + 1)] = spread(p + [-m for m in q], sp1[...])
            t1[1, :, 768 * h : 768 * (h + 1)] = spread(q + p, sp1[...])
        plus = [plane(19 + n) for n in range(5)]
        minus = [plane(24 + n) for n in range(5)]
        for h in range(2):
            p, q = plus[2 * h : 2 * h + 3], minus[2 * h : 2 * h + 3]
            t2[0, :, 640 * h : 640 * (h + 1)] = spread(p + [-m for m in q], sp2[h])
            t2[1, :, 640 * h : 640 * (h + 1)] = spread(q + p, sp2[h])


def forward(counts, sources, picked, parts, table, sp, after):
    sets = len(counts)
    one = (
        jax.ShapeDtypeStruct((EDGES, 64 * ROWS0), BF16),
        jax.ShapeDtypeStruct((2, EDGES, 64 * ROWS1), BF16),
        jax.ShapeDtypeStruct((2, EDGES, 64 * ROWS2), BF16),
    )
    outs = pl.pallas_call(
        functools.partial(forward_kernel, sets, len(parts)),
        out_shape=one * sets,
        in_specs=[SMEM] * (3 * sets) + [HBM] * (len(parts) + 4) + [ANY],
        out_specs=(VMEM,) * (3 * sets),
        scratch_shapes=[
            pltpu.VMEM((sets, KP * PITCH, LANES), F32),
            pltpu.VMEM((len(parts) * parts[0].shape[0], JP, LANES), BF16),
            pltpu.VMEM((ROTS, KP, JP), BF16),
        ]
        + [pltpu.VMEM(m.shape, BF16) for m in sp]
        + [pltpu.SemaphoreType.DMA((len(parts) + 4,))],
        compiler_params=WIDE,
    )(*counts, *sources, *picked, *parts, table, *sp, after)
    return [outs[3 * i : 3 * i + 3] for i in range(sets)]


def back_kernel(sets, trash, finish, *refs):
    counts, picked, targets = refs[0:sets], refs[sets : 2 * sets], refs[2 * sets : 3 * sets]
    refs = refs[3 * sets :]
    sources = [refs[3 * i : 3 * i + 3] for i in range(sets)]
    table, gathered, _ = refs[3 * sets : 3 * sets + 3]
    refs = refs[3 * sets + 3 :]
    outs, (w0, w1, w2, t0, t1, t2, rot_ref, tmp, acc, sems) = refs[:-10], refs[-10:]
    moves = []
    start = 0
    for n, (weight, turned, size) in enumerate(((w0, t0, G0), (w1, t1, G1), (w2, t2, G2))):
        moves.append([(sources[i][n], turned.at[i]) for i in range(sets)])
        moves[-1].append((gathered.at[:, pl.ds(start, size), :], weight))
        start += size
    moves.append([(table, rot_ref)])
    copies = []
    for n, group in enumerate(moves):
        copies.append(
            [pltpu.make_async_copy(src, dst, sems.at[n, m]) for m, (src, dst) in enumerate(group)]
        )
        for copy in copies[-1]:
            copy.start()

    def arrived(n):
        for copy in copies[n]:
            copy.wait()

    acc[...] = jnp.zeros_like(acc)
    for i in range(sets):
        tmp[i, pl.ds(KEPT * PITCH, (KP - KEPT) * PITCH), :] = jnp.zeros(((KP - KEPT) * PITCH, LANES), F32)

    def mix(lhs, ref, rows, blocks, places):
        for b in range(0, blocks, 2):
            width = min(2, blocks - b)
            weight = [
                ref[:, (b + i) * rows : (b + i + 1) * rows, :].reshape(16 * rows, LANES) for i in range(width)
            ]
            weight = jnp.concatenate(weight, axis=1) if width == 2 else weight[0]
            result = jnp.dot(lhs, weight, preferred_element_type=F32)
            for n, (i, first) in enumerate(places):
                for w in range(width):
                    tmp[i, pl.ds((first + b + w) * PITCH, EDGES), :] = result[
                        n * EDGES : (n + 1) * EDGES, w * LANES : (w + 1) * LANES
                    ]

    arrived(0)
    mix(t0[...].reshape(sets * EDGES, 64 * ROWS0), w0, 4 * ROWS0, BLK0, [(i, 0) for i in range(sets)])
    for n, (lhs, ref, rows, blocks, first) in enumerate(((t1, w1, ROWS1, BLK1, 7), (t2, w2, ROWS2, BLK2, 19))):
        arrived(n + 1)
        mix(
            lhs[...].reshape(sets * 2 * EDGES, 64 * rows), ref, 4 * rows, blocks,
            [(i, first + sign * blocks) for i in range(sets) for sign in range(2)],
        )
    arrived(3)

    for i in range(sets):
        count = counts[i][0]

        def step(s, carry, i=i, count=count):
            for u in range(STEP):
                e = s * STEP + u
                rows = tmp[i, pl.ds(e, KP, stride=PITCH), :].astype(BF16)
                part = lax.dot_general(
                    rot_ref[picked[i][e]], rows, (((0,), (0,)), ((), ())), preferred_element_type=F32
                )
                acc[jnp.where(e < count, targets[i][e], trash)] += part
            return carry

        lax.fori_loop(0, blocks_of(count), step, 0)
    finish(acc, *outs)


def store_returned(acc, first, middle, last):
    first[...] = acc[0:36].astype(BF16)
    middle[...] = acc[36:72]
    last[...] = acc[72:108].astype(BF16)


def store_gathered(acc, out):
    out[...] = acc[0:ATOMS]


def back(counts, picked, targets, turned, table, gathered, after, rows, trash, finish, out_shape):
    sets = len(counts)
    return pl.pallas_call(
        functools.partial(back_kernel, sets, trash, finish),
        out_shape=out_shape,
        in_specs=[SMEM] * (3 * sets) + [HBM] * (3 * sets + 2) + [ANY],
        out_specs=jax.tree.map(lambda _: VMEM, out_shape),
        scratch_shapes=[
            pltpu.VMEM((16, G0, LANES), BF16),
            pltpu.VMEM((16, G1, LANES), BF16),
            pltpu.VMEM((16, G2, LANES), BF16),
            pltpu.VMEM((sets, EDGES, 64 * ROWS0), BF16),
            pltpu.VMEM((sets, 2, EDGES, 64 * ROWS1), BF16),
            pltpu.VMEM((sets, 2, EDGES, 64 * ROWS2), BF16),
            pltpu.VMEM((ROTS, KP, JP), BF16),
            pltpu.VMEM((sets, KP * PITCH, LANES), F32),
            pltpu.VMEM((rows, JP, LANES), F32),
            pltpu.SemaphoreType.DMA((4, sets + 1)),
        ],
        compiler_params=WIDE,
    )(*counts, *picked, *targets, *[t for one in turned for t in one], table, gathered, after)


def final_kernel(border_atoms, feats, gathered, returned, out, acc):
    for a in range(ATOMS):
        acc[pl.ds(a * 57, JP), :] = gathered[a]
    for t in range(BOUND):
        acc[pl.ds(border_atoms[t] * 57, JP), :] += returned[t]
    for j in range(HARM):
        total = acc[pl.ds(j, ATOMS, stride=57), :]
        out[j] = (feats[j].astype(F32) + 0.25 * total).astype(BF16)


def swap(axis, block, odd):
    count = lax.axis_size(axis)
    return lax.ppermute(block, axis, [(i, (i + (1 if (i + odd) % 2 == 0 else -1)) % count) for i in range(count)])


def exchange(axis, first, last):
    last = swap(axis, last, 1)
    if axis == GY:
        both = lax.all_gather(first, "core", axis=0, tiled=False)
        return jnp.where(lax.axis_index("core") == 0, both[1], both[0]), last
    return swap(axis, first, 0), last


def widen(axis, block):
    first, last = exchange(axis, block, block)
    return jnp.concatenate([first, block, last], axis=0)


def fold(axis, first, middle, last):
    first, last = exchange(axis, first, last)
    return middle + first.astype(F32) + last.astype(F32)


def thirds(block):
    third = block.shape[0] // 3
    return block[:third].astype(BF16), block[third : 2 * third], block[2 * third :].astype(BF16)


GX, GY, GZ = "gx", ("zh", "core"), ("x", "zl")


def shards(
    features,
    border_atoms,
    inner_source,
    inner_target,
    inner_rotation,
    inner_count,
    cross_source,
    cross_target,
    cross_rotation,
    cross_count,
    rotations,
    order_zero,
    order_one,
    order_two,
):
    share = pl.pallas_call(
        share_kernel,
        out_shape=jax.ShapeDtypeStruct((ROWS0 * BLK0 + ROWS1 * BLK1 + ROWS2 * BLK2, LANES), BF16),
        in_specs=[VMEM] * 3,
        out_specs=VMEM,
        compiler_params=WIDE,
    )(order_zero, order_one.transpose(1, 0, 2), order_two.transpose(1, 0, 2))
    four = lax.all_gather(share, "x", axis=0, tiled=False)
    pieces = []
    start = 0
    for rows, blocks in ((ROWS0, BLK0), (ROWS1, BLK1), (ROWS2, BLK2)):
        piece = four[:, start : start + rows * blocks].reshape(4, blocks, rows, LANES)
        pieces.append(piece.transpose(1, 0, 2, 3).reshape(blocks * 4 * rows, LANES))
        start += rows * blocks
    gathered_weights = lax.all_gather(jnp.concatenate(pieces, axis=0), ("zh", "zl", "core"), axis=0, tiled=False)

    feats = features[0, 0, 0].transpose(1, 0, 2)
    border_rows = border_atoms[0, 0, 0]
    x, border = pl.pallas_call(
        tables_kernel,
        out_shape=(
            jax.ShapeDtypeStruct((ATOMS, JP, LANES), BF16),
            jax.ShapeDtypeStruct((BOUND, JP, LANES), BF16),
        ),
        in_specs=[SMEM, VMEM],
        out_specs=(VMEM, VMEM),
        scratch_shapes=[pltpu.VMEM((HARM * 33, LANES), F32)],
        compiler_params=PARAMS,
    )(border_rows, feats)

    table = pl.pallas_call(
        rotations_kernel,
        out_shape=jax.ShapeDtypeStruct((ROTS, KP, JP), BF16),
        in_specs=[VMEM],
        out_specs=VMEM,
        scratch_shapes=[pltpu.VMEM((ROTS * (KP + 1), LANES), F32)],
        compiler_params=pltpu.CompilerParams(vmem_limit_bytes=12 * 2**20),
    )(rotations)

    sp = spreads()
    count_in, count_x = inner_count.reshape(1), cross_count.reshape(1)
    source_in, target_in, rot_in = inner_source[0, 0, 0], inner_target[0, 0, 0], inner_rotation[0, 0, 0]
    far_rows, target_x = cross_source[0, 0, 0], cross_target[0, 0, 0]
    rot_inward, rot_outward = cross_rotation[0, 0, 0, 0], cross_rotation[0, 0, 0, 1]
    def place(axis, offset):
        return jnp.where(lax.axis_index(axis) % 2 == 1, offset, 2 - offset)

    slot, atom = far_rows // BOUND, far_rows % BOUND
    on_x, on_y, on_z = place(GX, slot // 9), place(GY, slot // 3 % 3), place(GZ, slot % 3)
    far_rows = ((on_x * 3 + on_y) * 3 + on_z) * BOUND + atom
    fold_rows = ((on_x * 3 + on_z) * 3 + on_y) * BOUND + atom

    near = widen(GY, widen(GZ, border))
    near, table = lax.optimization_barrier((near, table))
    near_first, near_last = exchange(GX, near, near)
    turned_out, turned_in = forward(
        [count_x, count_in], [target_x, source_in], [rot_outward, rot_in], [x], table, sp, near
    )
    [turned_x] = forward(
        [count_x], [far_rows], [rot_inward], [near_first, near, near_last], table, sp, turned_in[0]
    )

    face = (36, JP, LANES)
    first, middle, last = back(
        [count_x], [rot_outward], [fold_rows], [turned_out], table, gathered_weights, turned_x[0], 112, AROUND,
        store_returned,
        (jax.ShapeDtypeStruct(face, BF16), jax.ShapeDtypeStruct(face, F32), jax.ShapeDtypeStruct(face, BF16)),
    )
    gathered = back(
        [count_in, count_x], [rot_in, rot_inward], [target_in, target_x], [turned_in, turned_x], table,
        gathered_weights, first, 40, ATOMS, store_gathered, jax.ShapeDtypeStruct((ATOMS, JP, LANES), F32),
    )
    returned = fold(GX, first, middle, last)
    returned, gathered = lax.optimization_barrier((returned, gathered))
    returned = fold(GZ, *thirds(returned))
    returned = fold(GY, *thirds(returned))

    updated = pl.pallas_call(
        final_kernel,
        out_shape=jax.ShapeDtypeStruct((HARM, ATOMS, LANES), BF16),
        in_specs=[SMEM] + [VMEM] * 3,
        out_specs=VMEM,
        scratch_shapes=[pltpu.VMEM((ATOMS * 57, LANES), F32)],
        compiler_params=PARAMS,
    )(border_rows, feats, gathered, returned)
    return updated.transpose(1, 0, 2).reshape(features.shape)


def solution(mesh):
    fine = Mesh(mesh.devices.reshape(8, 4, 2, 4, 2), ("gx", "zh", "core", "x", "zl"))
    cell = ("gx", GY, GZ)
    plane = GY + GZ
    in_specs = (
        P(*cell, None, None, None),
        P(*cell, None),
        P(*cell, None),
        P(*cell, None),
        P(*cell, None),
        P(*cell),
        P(*cell, None),
        P(*cell, None),
        P(*cell, None, None),
        P(*cell),
        P(),
        P(plane, None),
        P(None, plane, None),
        P(None, plane, None),
    )
    out_specs = P(*cell, None, None, None)
    return jax.shard_map(shards, mesh=fine, in_specs=in_specs, out_specs=out_specs, check_vma=False)
```
